128 devices in a mesh: dp: 4 (over z), samp: 32 (over x, y, core).
Axes of the slice: x: 4, y: 4, z: 4, core: 2. Of those that a mesh axis runs over, the one named last changes fastest.
Arguments:
- prompt_kv: bfloat16 [4, 512, 2, 4096], P('dp', 'samp'), may hold values from -6 to 6
- queries: bfloat16 [4, 96, 256, 2048], P('dp', 'samp')
- completion_kv: bfloat16 [4, 96, 256, 4096], P('dp', 'samp')
- out_grad: bfloat16 [4, 96, 256, 2048], P('dp', 'samp'), may hold values from -96 to 96
- rewards: float32 [4, 96], P('dp', 'samp'), may hold values from 0 to 1
- token_mask: int32 [4, 96, 256], P('dp', 'samp'), may hold values 0 or 1
- sample_lists: int32 [4, 32, 3], P('dp'), may hold values from -1 to 1, as said below
- prompt_samples: int32 [4, 2], P('dp'), may hold values from 1 to 95, as said below
Outputs:
- query_grad: bfloat16 [4, 96, 256, 2048], P('dp', 'samp')
- completion_grad: bfloat16 [4, 96, 256, 4096], P('dp', 'samp')
- prompt_grad: float32 [4, 512, 2, 4096], P('dp', 'samp')
The draws below stay inside these ranges and needn't reach their ends.
Inputs may be any that keep to these rules, and one draw needn't show every extreme that they name: `sample_lists`: row i lists the prompts of the 3 slots of device i of the group. Live slots come first and -1 marks an empty slot. Every device has a live slot, some device of each group has all 3 live, every prompt has a live slot, and in some group every slot is live and one prompt has all but one of them. `prompt_samples`: the number of live slots of the group that name the prompt.
All inputs are finite; a program needn't handle non-finite values. No bound on the sum of `token_mask` on one device may be relied on, other than what follows from the above.
Results may differ from the reference program's by a relative error of at most 0.0015.
The reference program's roundings to bfloat16 on the way (of `weighted`, `keys_all`, `probs_low` and `dscore`) count: a program that leaves them out, or rounds other values in their place, can miss the bound.
Values may be sent and summed in bfloat16 or wider, within the bound.
No kernel may reach another device: no remote copies, remote signals or barrier semaphores. Data moves between devices by JAX's collectives and lax.ppermute only.
A program may use at most 320 MiB of HBM per device.

```python
import jax
import jax.numpy as jnp
from jax import lax

HEADS = 16
HD = 128
LP = 512
LC = 256
CAP = 3
PROMPTS = 2
GROUPS = 4
SLOTS = 96
N_SAMP = 32


def completion_base(key):
    return jax.random.normal(key, (GROUPS, SLOTS, LC, 2 * HEADS * HD), jnp.float32)


def slot_table(key):
    key_counts, key_full, key_prompt, key_hot = jax.random.split(key, 4)
    counts = jax.random.randint(key_counts, (GROUPS, N_SAMP), 1, CAP + 1)
    full_dev = jax.random.randint(key_full, (GROUPS, 1), 0, N_SAMP)
    hot_group = jax.random.randint(key_hot, (), 0, GROUPS)
    dev_pos = jnp.arange(N_SAMP, dtype=jnp.int32)
    group_pos = jnp.arange(GROUPS, dtype=jnp.int32)
    is_hot = group_pos[:, None] == hot_group
    counts = jnp.where(dev_pos[None, :] == full_dev, CAP, counts)
    counts = jnp.where(is_hot, CAP, counts)
    prompt_pick = jax.random.randint(key_prompt, (GROUPS, N_SAMP, CAP), 0, PROMPTS)
    prompt_pick = jnp.where(is_hot[:, :, None], 0 * prompt_pick, prompt_pick)
    slot_pos = jnp.arange(CAP, dtype=jnp.int32)
    forced = (slot_pos[None, None, :] == 0) & (dev_pos[None, :, None] < PROMPTS)
    prompt_pick = jnp.where(forced, dev_pos[None, :, None] + 0 * prompt_pick, prompt_pick)
    return jnp.where(slot_pos[None, None, :] < counts[:, :, None], prompt_pick, -1).astype(jnp.int32)


def draw_completion_kv(key, part):
    shared_base = completion_base(key)
    return shared_base.astype(jnp.bfloat16)


def draw_queries(key, part):
    key = jax.random.fold_in(key, 5)
    normal_part = jax.random.normal(key, (GROUPS, SLOTS, LC, HEADS * HD), jnp.float32)
    return normal_part.astype(jnp.bfloat16)


def draw_sample_lists(key, part):
    slot_lists = slot_table(key)
    return slot_lists


def draw_prompt_samples(key, part):
    slot_lists = slot_table(key)
    matches = slot_lists[:, :, :, None] == jnp.arange(PROMPTS, dtype=jnp.int32)[None, None, None, :]
    return jnp.sum(matches.astype(jnp.int32), axis=(1, 2)).astype(jnp.int32)


def place_ends(array, rng, least, top_value):
    place = [jax.random.randint(jax.random.fold_in(rng, axis), (), 0, length) for axis, length in enumerate(array.shape)]
    main_axis = array.shape.index(max(array.shape))
    neighbour = place[:main_axis] + [(place[main_axis] + 1) % array.shape[main_axis]] + place[main_axis + 1:]
    return array.at[tuple(place)].set(least).at[tuple(neighbour)].set(top_value)


def level_of(rng, extent, cuts, low, top_value):
    def one(dim, blocks):
        steps = jax.random.uniform(jax.random.fold_in(jax.random.fold_in(rng, 6), dim), (blocks,), jnp.float32, low / len(cuts), top_value / len(cuts))
        return jnp.repeat(jnp.exp(steps), extent[dim] // blocks).reshape((-1,) + (1,) * (len(extent) - dim - 1))

    level = one(*cuts[0])
    for cut in cuts[1:]:
        level = level * one(*cut)
    return level


def scatter_about(key, shape, deviation, most, cuts=(), held_as=jnp.bfloat16):
    values = deviation * jax.random.normal(key, shape, jnp.float32)
    if cuts:
        values = values * level_of(key, shape, cuts, -0.22, 0.18)
    return jnp.clip(values, -most, most).astype(held_as)


def setup_inputs(seed: int = 0) -> dict:
    arg_keys = jax.random.split(jax.random.key(seed), 9)
    return {
        "prompt_kv": scatter_about(arg_keys[0], (GROUPS, LP, PROMPTS, 2 * HEADS * HD), 1.0, 6.0, ((0, 4), (1, 32))),
        "queries": draw_queries(jax.random.fold_in(arg_keys[8], 71), 0),
        "completion_kv": draw_completion_kv(jax.random.fold_in(arg_keys[8], 71), 0),
        "out_grad": scatter_about(arg_keys[3], (GROUPS, SLOTS, LC, HEADS * HD), 16.0, 96.0, ((0, 4), (1, 32))),
        "rewards": jnp.clip(1.0 * jax.random.uniform(arg_keys[4], (GROUPS, SLOTS), jnp.float32) ** level_of(arg_keys[4], (GROUPS, SLOTS), ((0, 4), (1, 32)), -0.2, 0.2), 0.0, 1.0),
        "token_mask": place_ends((jax.random.randint(arg_keys[5], (GROUPS, SLOTS, LC), 0, 2) < 1).astype(jnp.int32), jax.random.fold_in(arg_keys[5], 1), 0, 1),
        "sample_lists": draw_sample_lists(jax.random.fold_in(arg_keys[8], 71), 0),
        "prompt_samples": draw_prompt_samples(jax.random.fold_in(arg_keys[8], 71), 0),
    }


def slot_backward(query_rows, keys_all, values_all, grad_rows):
    score_scale = HD ** -0.5
    key_len = keys_all.shape[0]
    query_heads = query_rows.astype(jnp.float32).reshape(LC, HEADS, HD)
    key_heads = keys_all.astype(jnp.float32).reshape(key_len, HEADS, HD)
    value_heads = values_all.astype(jnp.float32).reshape(key_len, HEADS, HD)
    grad_heads = grad_rows.astype(jnp.float32).reshape(LC, HEADS, HD)
    scores = jnp.einsum("qhd,khd->hqk", query_heads, key_heads) * score_scale
    row_peak = jnp.max(scores, axis=-1, keepdims=True)
    raised = jnp.exp(scores - row_peak)
    prob_full = raised / jnp.sum(raised, axis=-1, keepdims=True)
    probs_low = prob_full.astype(jnp.bfloat16).astype(jnp.float32)
    attended = jnp.einsum("hqk,khd->qhd", probs_low, value_heads)
    row_dot = jnp.sum(grad_heads * attended, axis=-1)
    dprob = jnp.einsum("qhd,khd->hqk", grad_heads, value_heads)
    dscore = (prob_full * (dprob - jnp.transpose(row_dot)[:, :, None])).astype(jnp.bfloat16).astype(jnp.float32)
    dquery = jnp.einsum("hqk,khd->qhd", dscore, key_heads) * score_scale
    dkeys = jnp.einsum("hqk,qhd->khd", dscore, query_heads) * score_scale
    dvalues = jnp.einsum("hqk,qhd->khd", probs_low, grad_heads)
    return dquery.reshape(LC, HEADS * HD), dkeys.reshape(key_len, HEADS * HD), dvalues.reshape(key_len, HEADS * HD)


def reference(prompt_kv, queries, completion_kv, out_grad, rewards, token_mask, sample_lists, prompt_samples):
    feat_width = HEADS * HD
    slot_lists = sample_lists.reshape(GROUPS, SLOTS)
    slot_live = slot_lists >= 0
    prompt_ids = jnp.maximum(slot_lists, 0).astype(jnp.int32)
    onehot = ((prompt_ids[:, :, None] == jnp.arange(PROMPTS, dtype=jnp.int32)[None, None, :]) & slot_live[:, :, None]).astype(jnp.float32)
    reward_sum = jnp.sum(onehot * rewards[:, :, None], axis=1)
    reward_mean = reward_sum / prompt_samples.astype(jnp.float32)
    advantage = rewards - jnp.sum(onehot * reward_mean[:, None, :], axis=2)
    masked_all = jnp.sum(jnp.where(slot_live[:, :, None], token_mask, 0)).astype(jnp.float32)
    live_all = jnp.sum(slot_live.astype(jnp.float32))
    factor = LC * live_all / masked_all
    weights = token_mask.astype(jnp.float32) * advantage[:, :, None] * factor
    weighted = (out_grad.astype(jnp.float32) * weights[..., None]).astype(jnp.bfloat16)

    query_list = []
    comp_list = []
    prompt_list = []
    for group_idx in range(GROUPS):
        prompt_table = prompt_kv[group_idx]

        def visit(prompt_sum, slot_items):
            query_rows, comp_rows, grad_rows, live_flag, prompt = slot_items

            def active():
                prompt_rows = lax.dynamic_index_in_dim(prompt_table, prompt, 1, keepdims=False)
                keys_all = jnp.concatenate([prompt_rows[:, :feat_width], comp_rows[:, :feat_width]], axis=0)
                values_all = jnp.concatenate([prompt_rows[:, feat_width:], comp_rows[:, feat_width:]], axis=0)
                dquery, dkeys, dvalues = slot_backward(query_rows, keys_all, values_all, grad_rows)
                return (dquery, jnp.concatenate([dkeys[LP:], dvalues[LP:]], axis=1),
                        jnp.concatenate([dkeys[:LP], dvalues[:LP]], axis=1))

            def spare():
                return (jnp.zeros((LC, feat_width), jnp.float32), jnp.zeros((LC, 2 * feat_width), jnp.float32),
                        jnp.zeros((LP, 2 * feat_width), jnp.float32))

            dquery, dcomp, dprompt = lax.cond(live_flag, active, spare)
            current = lax.dynamic_index_in_dim(prompt_sum, prompt, 1, keepdims=True)
            prompt_sum = lax.dynamic_update_slice_in_dim(prompt_sum, current + dprompt[:, None, :], prompt, 1)
            return prompt_sum, (dquery.astype(jnp.bfloat16), dcomp.astype(jnp.bfloat16))

        start_sum = jnp.zeros((LP, PROMPTS, 2 * feat_width), jnp.float32)
        prompt_sum, outputs = lax.scan(visit, start_sum, (queries[group_idx], completion_kv[group_idx], weighted[group_idx], slot_live[group_idx], prompt_ids[group_idx]))
        query_list.append(outputs[0])
        comp_list.append(outputs[1])
        prompt_list.append(prompt_sum)
    return jnp.stack(query_list), jnp.stack(comp_list), jnp.stack(prompt_list)
```

```python
import functools
import math

import jax
import jax.numpy as jnp
from jax import lax
from jax.experimental import pallas as pl
from jax.experimental.pallas import tpu as pltpu
from jax.sharding import PartitionSpec as P

HD = 128
NX, NY, NC = 4, 4, 2
CHUNKS = (3, 3, 2)
BLOCKS = NX * NY
STEPS = 32760.0
F32 = jnp.float32
BF16 = jnp.bfloat16
I16 = jnp.int16


def shift_pairs(dx, dy, dc):
    pairs = []
    for x in range(NX):
        for y in range(NY):
            for c in range(NC):
                to_x, to_y, to_c = (x + dx) % NX, (y + dy) % NY, (c + dc) % NC
                pairs.append(((x * NY + y) * NC + c, (to_x * NY + to_y) * NC + to_c))
    return pairs


def move_core(value):
    return lax.ppermute(value, "samp", shift_pairs(0, 0, 1))


def move_axis(value, axis, step):
    if axis == "x":
        return lax.ppermute(value, "samp", shift_pairs(step, 0, 0))
    if axis == "y":
        return lax.ppermute(value, "samp", shift_pairs(0, step, 0))
    return lax.ppermute(value, "dp", [(i, (i + step) % 4) for i in range(4)])


def gather_axis(value, axis):
    return [value] + [move_axis(value, axis, step) for step in (1, 2, 3)]


def sum_axis(value, axis):
    first, second, third, fourth = gather_axis(value, axis)
    return (first + second) + (third + fourth)


def to_steps(value):
    peak = jnp.max(jnp.max(jnp.abs(value), axis=0, keepdims=True), axis=1, keepdims=True)
    code = jnp.floor(jnp.log2(jnp.clip(peak, 1e-30, 1e30))) + 1.0
    steps = jnp.floor(value * (jnp.exp2(-code) * STEPS) + 0.5)
    return steps.astype(jnp.int32).astype(I16), code


def code_rows(codes, rows):
    return jnp.broadcast_to(codes[:1], (rows, HD)).astype(jnp.int32).astype(I16)


def backward_pair(prompt, live, query, comp_k, comp_v, grad, weight, prompt_refs, blocks, grad_ref):
    scale = HD**-0.5
    base2 = scale * math.log2(math.e)
    nt = (((1,), (1,)), ((), ()))
    tn = (((0,), (0,)), ((), ()))
    nn = (((1,), (0,)), ((), ()))

    def dot(a, b, dims):
        return lax.dot_general(a, b, dims, preferred_element_type=F32)

    key_col = pl.multiple_of(prompt * (2 * HD), 2 * HD)
    val_col = pl.multiple_of(prompt * (2 * HD) + HD, HD)
    size = prompt_refs[0].shape[0] * len(prompt_refs) // BLOCKS

    def prompt_rows(col):
        parts = []
        for block in blocks:
            ref, place = prompt_refs[block // NX], block % NX
            parts.append(ref[place * size : (place + 1) * size, pl.ds(col, HD)])
        return jnp.concatenate(parts, axis=0)

    prompt_k, prompt_v = prompt_rows(key_col), prompt_rows(val_col)
    query = jnp.where(live, query, jnp.zeros_like(query))
    weighted = (grad.astype(F32) * weight).astype(BF16)
    weighted = jnp.where(live, weighted, jnp.zeros_like(weighted))

    s_p = dot(prompt_k, query, nt)
    s_c = dot(comp_k, query, nt)
    peak = jnp.maximum(jnp.max(s_p, axis=0, keepdims=True), jnp.max(s_c, axis=0, keepdims=True))
    peak = peak * base2
    e_p = jnp.exp2(s_p * base2 - peak)
    e_c = jnp.exp2(s_c * base2 - peak)
    total = jnp.sum(e_p, axis=0, keepdims=True) + jnp.sum(e_c, axis=0, keepdims=True)
    inverse = 1.0 / total
    p_p = e_p * inverse
    p_c = e_c * inverse
    low_p = p_p.astype(BF16)
    low_c = p_c.astype(BF16)
    d_p = dot(prompt_v, weighted, nt)
    d_c = dot(comp_v, weighted, nt)
    row_dot = jnp.sum(low_p.astype(F32) * d_p, axis=0, keepdims=True) + jnp.sum(
        low_c.astype(F32) * d_c, axis=0, keepdims=True
    )
    ds_p = (p_p * (d_p - row_dot)).astype(BF16)
    ds_c = (p_c * (d_c - row_dot)).astype(BF16)
    dv_p = dot(low_p, weighted, nn)
    dk_p = dot(ds_p, query, nn) * scale
    grad_ref[:, pl.ds(key_col, HD)] += dk_p
    grad_ref[:, pl.ds(val_col, HD)] += dv_p
    dk_c = (dot(ds_c, query, nn) * scale).astype(BF16)
    dv_c = dot(low_c, weighted, nn).astype(BF16)
    dq = ((dot(ds_p, prompt_k, tn) + dot(ds_c, comp_k, tn)) * scale).astype(BF16)
    return dq, dk_c, dv_c


def chunk_kernel(
    blocks, info, q0, k0, v0, g0, q1, k1, v1, g1, w_ref, *rest
):
    prompt_refs, (out0, out1, kept, *sent, grad_ref, codes_ref) = rest[:NX], rest[NX:]
    head, slot = pl.program_id(0), pl.program_id(1)

    @pl.when(slot == 0)
    def _():
        grad_ref[...] = jnp.zeros_like(grad_ref)

    @pl.when((slot == 0) & (head == 0))
    def _():
        codes_ref[...] = jnp.zeros_like(codes_ref)

    slots = w_ref.shape[0] // 2
    for half, (q, k, v, g, out) in enumerate(((q0, k0, v0, g0, out0), (q1, k1, v1, g1, out1))):
        entry = info[1 + half * slots + slot]
        results = backward_pair(
            jnp.maximum(entry, 0),
            entry >= 0,
            q[0],
            k[0],
            v[0],
            g[0],
            w_ref[half * slots + slot],
            prompt_refs,
            blocks,
            grad_ref,
        )
        for index, value in enumerate(results):
            out[0, index] = value

    rows = kept.shape[0]

    @pl.when(slot == slots - 1)
    def _():
        kept[...] = grad_ref[:rows]
        lane = lax.broadcasted_iota(jnp.int32, (8, HD), 1)
        for index, ref in enumerate(sent):
            part = slice((index + 1) * rows, (index + 2) * rows)
            codes = codes_ref[index]
            for tile in range(4):
                value, code = to_steps(grad_ref[part, tile * HD : (tile + 1) * HD])
                ref[:, pl.ds(pl.multiple_of(head * (4 * HD) + tile * HD, HD), HD)] = value
                codes = jnp.where(lane == head * 4 + tile, code, codes)
            codes_ref[index] = codes
            rest_cols = ref.shape[1] - HD
            ref[:, rest_cols:] = code_rows(codes, rows)


def chunk_backward(first, heads, place, blocks, info, queries, comp, grads, other, weights, prompt_parts):
    slots, length, width = queries.shape
    half = width // HD // 2
    rows = prompt_parts[0].shape[0]
    keys = rows * NX

    def own(offset):
        return pl.BlockSpec(
            (1, length, HD), lambda h, s, info: (s, 0, offset + info[0] * half + first + h)
        )

    def sent(offset):
        return pl.BlockSpec((1, length, HD), lambda h, s, info: (s, 0, offset * half + first + h))

    result = pl.BlockSpec((1, 3, length, HD), lambda h, s, info: (s, 0, 0, h))
    cols = heads * 4 * HD + HD
    piece = pl.BlockSpec((rows, cols), lambda h, s, info: (0, 0))
    kept = pl.BlockSpec((rows, 4 * HD), lambda h, s, info: (0, h))
    grid_spec = pltpu.PrefetchScalarGridSpec(
        num_scalar_prefetch=1,
        grid=(heads, slots),
        in_specs=[
            own(0),
            own(0),
            own(2 * half),
            own(0),
            sent(0),
            sent(1),
            sent(2),
            sent(3),
            pl.BlockSpec(weights.shape, lambda h, s, info: (0, 0, 0)),
        ]
        + [pl.BlockSpec((rows, 4 * HD), lambda h, s, info: (0, place + h))] * NX,
        scratch_shapes=[pltpu.VMEM((keys, 4 * HD), F32), pltpu.VMEM((NX - 1, 8, HD), F32)],
        out_specs=[result, result, kept] + [piece] * (NX - 1),
    )
    slot_shape = jax.ShapeDtypeStruct((slots, 3, length, heads * HD), BF16)
    kept_shape = jax.ShapeDtypeStruct((rows, heads * 4 * HD), F32)
    piece_shape = jax.ShapeDtypeStruct((rows, cols), I16)
    count = heads * slots * 2
    return pl.pallas_call(
        functools.partial(chunk_kernel, blocks),
        grid_spec=grid_spec,
        out_shape=[slot_shape, slot_shape, kept_shape] + [piece_shape] * (NX - 1),
        compiler_params=pltpu.CompilerParams(
            dimension_semantics=("arbitrary", "arbitrary"), vmem_limit_bytes=48 * 1024 * 1024
        ),
        cost_estimate=pl.CostEstimate(
            flops=count * 24 * (keys + length) * length * HD,
            bytes_accessed=count * 7 * length * HD * 2 + heads * keys * 4 * HD * 6,
            transcendentals=count * (keys + length) * length,
        ),
        name="head_chunk",
    )(info, queries, comp, comp, grads, other, other, other, other, weights, *prompt_parts)


def place_kernel(core_ref, *refs):
    parts, (query_out, comp_out) = refs[:-2], refs[-2:]
    count = len(parts) // 2
    half = query_out.shape[2] // 2
    core = core_ref[0]

    def fill(out):
        for side, group in ((core, parts[:count]), (1 - core, parts[count:])):
            first = 0
            for part in group:
                size = part.shape[3]
                start = pl.multiple_of(side * half + first, HD)
                out[0, :, pl.ds(start, size)] = part[0, 0]
                first += size

    @pl.when(pl.program_id(1) == 0)
    def _():
        fill(query_out)

    @pl.when(pl.program_id(1) > 0)
    def _():
        fill(comp_out)


def place_slots(core, mine, got, width):
    slots, kinds, length, _ = mine[0].shape
    total = slots * kinds * length * width * 2
    return pl.pallas_call(
        place_kernel,
        grid=(slots, kinds),
        in_specs=[pl.BlockSpec(memory_space=pltpu.SMEM)]
        + [
            pl.BlockSpec((1, 1, length, part.shape[3]), lambda s, k: (s, k, 0, 0))
            for part in (*mine, *got)
        ],
        out_specs=[
            pl.BlockSpec((1, length, width), lambda s, k: (s, 0, 0)),
            pl.BlockSpec((1, length, width), lambda s, k: (s, 0, jnp.maximum(k - 1, 0))),
        ],
        out_shape=[
            jax.ShapeDtypeStruct((slots, length, width), BF16),
            jax.ShapeDtypeStruct((slots, length, 2 * width), BF16),
        ],
        cost_estimate=pl.CostEstimate(flops=0, bytes_accessed=2 * total, transcendentals=0),
        name="place_slots",
    )(core[None], *mine, *got)


def sum_kernel(counts, coded, *refs):
    ins, outs = refs[: 4 * len(counts)], refs[4 * len(counts) :]
    rows = outs[0].shape[0]
    lane = lax.broadcasted_iota(jnp.int32, (8, HD), 1)
    codes = [jnp.zeros((8, HD), F32) for _ in outs]
    place = 0
    for index, heads in enumerate(counts):
        kept, arrived = ins[4 * index], ins[4 * index + 1 : 4 * index + 4]
        scales = [jnp.exp2(ref[:16, heads * 4 * HD :].astype(F32)) * (1.0 / STEPS) for ref in arrived]
        for tile in range(4 * heads):
            cols = slice(tile * HD, (tile + 1) * HD)
            total = kept[:, cols]
            for ref, scale in zip(arrived, scales):
                total += ref[:, cols].astype(F32) * scale[:1, tile : tile + 1]
            for i, out in enumerate(outs):
                value = total[i * rows : (i + 1) * rows]
                if coded and i > 0:
                    value, code = to_steps(value)
                    codes[i] = jnp.where(lane == place, code, codes[i])
                out[:, place * HD : (place + 1) * HD] = value
            place += 1
    if coded:
        for out, code in zip(outs[1:], codes[1:]):
            out[:, place * HD :] = code_rows(code, rows)


def sum_parts(chunks, parts, coded):
    counts = [heads for heads, _, _ in chunks]
    ins = [value for _, kept, arrived in chunks for value in (kept, *arrived)]
    vmem = pl.BlockSpec(memory_space=pltpu.VMEM)
    rows, cols = ins[0].shape[0] // parts, sum(counts) * 4 * HD
    plain = jax.ShapeDtypeStruct((rows, cols), F32)
    other = jax.ShapeDtypeStruct((rows, cols + HD), I16) if coded else plain
    return pl.pallas_call(
        functools.partial(sum_kernel, counts, coded),
        in_specs=[vmem] * len(ins),
        out_specs=[vmem] * parts,
        out_shape=[plain] + [other] * (parts - 1),
        compiler_params=pltpu.CompilerParams(vmem_limit_bytes=32 * 1024 * 1024),
        cost_estimate=pl.CostEstimate(
            flops=0, bytes_accessed=rows * parts * cols * 14, transcendentals=0
        ),
        name="sum_parts",
    )(*ins)


def share_kernel(core_ref, mine_ref, got_ref, out_ref):
    core_first = core_ref[0] == 0
    heads = mine_ref.shape[1] // (4 * HD)
    for head in range(heads):
        for prompt in range(2):
            for kind in range(2):
                begin = (head * 4 + prompt * 2 + kind) * HD
                mine, got = mine_ref[:, begin : begin + HD], got_ref[:, begin : begin + HD]
                low, high = jnp.where(core_first, mine, got), jnp.where(core_first, got, mine)
                for side, value in enumerate((low, high)):
                    start = ((kind * 2 + side) * heads + head) * HD
                    out_ref[:, prompt, start : start + HD] = value


def place_share(core, mine, got):
    rows, width = mine.shape
    vmem = pl.BlockSpec(memory_space=pltpu.VMEM)
    return pl.pallas_call(
        share_kernel,
        in_specs=[pl.BlockSpec(memory_space=pltpu.SMEM), vmem, vmem],
        out_specs=vmem,
        out_shape=jax.ShapeDtypeStruct((rows, 2, width), F32),
        name="place_share",
    )(core[None], mine, got)


def three_parts(value):
    parts = []
    for _ in range(3):
        part = lax.reduce_precision(value, 8, 7)
        parts.append(part.astype(BF16))
        value = value - part
    return parts


def per_device(
    prompt_kv, queries, completion_kv, out_grad, rewards, token_mask, sample_lists, prompt_samples
):
    myself = lax.axis_index("samp")
    core = lax.rem(myself, 2)
    prompt_kv, queries, comp, grads = prompt_kv[0], queries[0], completion_kv[0], out_grad[0]
    slots, length, width = queries.shape
    half_width = width // 2
    half_heads = half_width // HD
    own_rows, prompts = prompt_kv.shape[0], prompt_kv.shape[1]

    lists_all = sample_lists[0]
    lists = jnp.concatenate(
        [
            lax.dynamic_index_in_dim(lists_all, myself, 0, keepdims=False),
            lax.dynamic_index_in_dim(lists_all, myself + 1 - 2 * core, 0, keepdims=False),
        ]
    )
    facts = jnp.concatenate(
        [token_mask[0].astype(F32), jnp.broadcast_to(rewards[0][:, None], (slots, length))], axis=0
    )
    facts_other = move_core(facts)
    masks = jnp.concatenate([facts[:slots], facts_other[:slots]], axis=0)
    reward = jnp.concatenate([facts[slots:, 0], facts_other[slots:, 0]])
    live = (lists >= 0).astype(F32)
    member = (lists[:, None] == jnp.arange(prompts, dtype=jnp.int32)[None, :]).astype(F32)
    counts = jnp.stack([jnp.sum(jnp.sum(masks, axis=1) * live), jnp.sum(live)])
    counts = sum_axis(jnp.broadcast_to(jnp.pad(counts, (0, 6))[:, None], (8, HD)), "dp")[:2, 0]
    stats = jnp.concatenate([jnp.sum(member * reward[:, None], axis=0), counts])
    stats = jnp.concatenate(three_parts(stats))
    stats = jnp.pad(stats[None, :], ((0, 2 * own_rows - 1), (0, HD - stats.shape[0])))

    kv_heads = prompt_kv.reshape(own_rows, prompts, 2, 2, half_heads, HD)
    kv_heads = jnp.transpose(kv_heads, (3, 0, 4, 1, 2, 5)).reshape(2, own_rows, -1)
    kv_mine = lax.dynamic_index_in_dim(kv_heads, core, 0, keepdims=False)
    kv_other = move_core(lax.dynamic_index_in_dim(kv_heads, 1 - core, 0, keepdims=False))
    block = jnp.concatenate([kv_mine, kv_other], axis=0)

    edge = CHUNKS[0] * 4 * HD
    early = jnp.concatenate([block[:, :edge], stats], axis=1)
    early = jnp.concatenate(gather_axis(early, "y"), axis=0)
    late = jnp.concatenate(gather_axis(block[:, edge:], "x"), axis=0)
    early = gather_axis(early, "x")

    def part(value, start):
        return lax.dynamic_slice_in_dim(value, start + (1 - core) * half_width, half_width, 2)

    sources, _, _ = lax.optimization_barrier(((queries, comp, grads), kv_other, counts))
    other = move_core(
        jnp.concatenate(
            [
                part(sources[0], 0),
                part(sources[1], 0),
                part(sources[1], width),
                part(sources[2], 0),
            ],
            axis=2,
        )
    )

    stats = jnp.sum(sum(value[:, edge:].astype(F32) for value in early), axis=0)
    stats = jnp.sum(stats[: 3 * (prompts + 2)].reshape(3, prompts + 2), axis=0)
    reward_mean = stats[:prompts] / prompt_samples[0].astype(F32)
    advantage = reward - jnp.sum(member * reward_mean[None, :], axis=1)
    factor = length * stats[prompts + 1] / stats[prompts]
    weights = masks * advantage[:, None] * factor
    weights = jnp.broadcast_to(weights[:, :, None], (2 * slots, length, HD))

    info = jnp.concatenate([core[None], lists]).astype(jnp.int32)
    info, late = lax.optimization_barrier((info, late))
    late = gather_axis(late, "y")
    straight = list(range(BLOCKS))
    turned = [i * NX + j for j in range(NX) for i in range(NY)]
    mine_parts, other_parts, waiting = [], [], []
    first = 0
    for heads in CHUNKS:
        early_chunk = first == 0
        outs = chunk_backward(
            first,
            heads,
            0 if early_chunk else first - CHUNKS[0],
            straight if early_chunk else turned,
            info,
            queries,
            comp,
            grads,
            other,
            weights,
            early if early_chunk else late,
        )
        first += heads
        mine, theirs, kept, *sent = outs
        if early_chunk:
            late, kept, sent, theirs = lax.optimization_barrier((late, kept, sent, theirs))
        else:
            count, *arrived = waiting.pop()
            arrived, moved, kept, sent, theirs = lax.optimization_barrier(
                (arrived, other_parts.pop(), kept, sent, theirs)
            )
            other_parts.append(moved)
            waiting.append((count, *arrived))
        info, _ = lax.optimization_barrier((info, kept))
        mine_parts.append(mine)
        arrived = [move_axis(value, "x", -step) for step, value in enumerate(sent, 1)]
        waiting.append((heads, kept, arrived))
        other_parts.append(move_core(theirs))

    query_out, comp_out = place_slots(core, mine_parts, other_parts, width)
    arrived = [arrived for _, _, arrived in waiting]
    arrived, query_out, comp_out = lax.optimization_barrier((arrived, query_out, comp_out))
    waiting = [(heads, kept, value) for (heads, kept, _), value in zip(waiting, arrived)]
    line = sum_parts(waiting, NY, True)
    back = [move_axis(line[step], "y", -step) for step in (1, 2, 3)]
    mine, theirs = sum_parts([(half_heads, line[0], back)], 2, False)
    share = place_share(core, mine, move_core(theirs))
    return (query_out[None], comp_out[None], share[None])


def solution(mesh):
    in_specs = (
        P("dp", "samp", None, None),
        P("dp", "samp", None, None),
        P("dp", "samp", None, None),
        P("dp", "samp", None, None),
        P("dp", "samp"),
        P("dp", "samp", None),
        P("dp", None, None),
        P("dp", None),
    )
    out_specs = (
        P("dp", "samp", None, None),
        P("dp", "samp", None, None),
        P("dp", "samp", None, None),
    )
    return jax.shard_map(
        per_device, mesh=mesh, in_specs=in_specs, out_specs=out_specs, check_vma=False
    )
```

```python
import functools
import math

import jax
import jax.numpy as jnp
from jax import lax
from jax.experimental import pallas as pl
from jax.experimental.pallas import tpu as pltpu
from jax.sharding import PartitionSpec as P

HD = 128
NX, NY, NC = 4, 4, 2
CHUNKS = (3, 3, 2)
BLOCKS = NX * NY
STEPS = 32760.0
STAGES = 5
VMEM_BYTES = 48 * 1024 * 1024
SMALL_BYTES = 32 * 1024 * 1024
MOST_BYTES = 60 * 1024 * 1024
F32 = jnp.float32
BF16 = jnp.bfloat16
I16 = jnp.int16


def shift_pairs(dx, dy, dc):
    pairs = []
    for x in range(NX):
        for y in range(NY):
            for c in range(NC):
                to_x, to_y, to_c = (x + dx) % NX, (y + dy) % NY, (c + dc) % NC
                pairs.append(((x * NY + y) * NC + c, (to_x * NY + to_y) * NC + to_c))
    return pairs


def move_core(value):
    return lax.ppermute(value, "samp", shift_pairs(0, 0, 1))


def move_axis(value, axis, step):
    if axis == "x":
        return lax.ppermute(value, "samp", shift_pairs(step, 0, 0))
    if axis == "y":
        return lax.ppermute(value, "samp", shift_pairs(0, step, 0))
    return lax.ppermute(value, "dp", [(i, (i + step) % 4) for i in range(4)])


def gather_axis(value, axis):
    return [value] + [move_axis(value, axis, step) for step in (1, 2, 3)]


def sum_axis(value, axis):
    first, second, third, fourth = gather_axis(value, axis)
    return (first + second) + (third + fourth)


def to_steps(value):
    peak = jnp.max(jnp.max(jnp.abs(value), axis=0, keepdims=True), axis=1, keepdims=True)
    code = jnp.floor(jnp.log2(jnp.clip(peak, 1e-30, 1e30))) + 1.0
    steps = jnp.floor(value * (jnp.exp2(-code) * STEPS) + 0.5)
    return steps.astype(jnp.int32).astype(I16), code


def code_rows(codes, rows):
    return jnp.broadcast_to(codes[:1], (rows, HD)).astype(jnp.int32).astype(I16)


def backward_pair(prompt, live, query, comp_k, comp_v, grad, weight, prompt_refs, blocks, grad_ref):
    scale = HD**-0.5
    base2 = scale * math.log2(math.e)
    nt = (((1,), (1,)), ((), ()))
    tn = (((0,), (0,)), ((), ()))
    nn = (((1,), (0,)), ((), ()))

    def dot(a, b, dims):
        return lax.dot_general(a, b, dims, preferred_element_type=F32)

    key_col = pl.multiple_of(prompt * (2 * HD), 2 * HD)
    val_col = pl.multiple_of(prompt * (2 * HD) + HD, HD)
    size = prompt_refs[0].shape[0] * len(prompt_refs) // BLOCKS

    def prompt_rows(col):
        parts = []
        for block in blocks:
            ref, place = prompt_refs[block // NX], block % NX
            parts.append(ref[place * size : (place + 1) * size, pl.ds(col, HD)])
        return jnp.concatenate(parts, axis=0)

    prompt_k, prompt_v = prompt_rows(key_col), prompt_rows(val_col)
    query = jnp.where(live, query, jnp.zeros_like(query))
    weighted = (grad.astype(F32) * weight).astype(BF16)
    weighted = jnp.where(live, weighted, jnp.zeros_like(weighted))

    s_p = dot(prompt_k, query, nt)
    s_c = dot(comp_k, query, nt)
    yield
    peak = jnp.maximum(jnp.max(s_p, axis=0, keepdims=True), jnp.max(s_c, axis=0, keepdims=True))
    peak = peak * base2
    e_p = jnp.exp2(s_p * base2 - peak)
    e_c = jnp.exp2(s_c * base2 - peak)
    total = jnp.sum(e_p, axis=0, keepdims=True) + jnp.sum(e_c, axis=0, keepdims=True)
    inverse = 1.0 / total
    p_p = e_p * inverse
    p_c = e_c * inverse
    low_p = p_p.astype(BF16)
    low_c = p_c.astype(BF16)
    yield
    d_p = dot(prompt_v, weighted, nt)
    d_c = dot(comp_v, weighted, nt)
    row_dot = jnp.sum(low_p.astype(F32) * d_p, axis=0, keepdims=True) + jnp.sum(
        low_c.astype(F32) * d_c, axis=0, keepdims=True
    )
    yield
    ds_p = (p_p * (d_p - row_dot)).astype(BF16)
    ds_c = (p_c * (d_c - row_dot)).astype(BF16)
    yield
    dv_p = dot(low_p, weighted, nn)
    dk_p = dot(ds_p, query, nn) * scale
    grad_ref[:, pl.ds(key_col, HD)] += dk_p
    grad_ref[:, pl.ds(val_col, HD)] += dv_p
    dk_c = (dot(ds_c, query, nn) * scale).astype(BF16)
    dv_c = dot(low_c, weighted, nn).astype(BF16)
    dq = ((dot(prompt_k, ds_p, tn) + dot(comp_k, ds_c, tn)) * scale).T.astype(BF16)
    return dq, dk_c, dv_c


def chunk_kernel(
    blocks, info, q0, k0, v0, g0, q1, k1, v1, g1, w_ref, *rest
):
    prompt_refs, (out0, out1, kept, *sent, grad_ref, codes_ref) = rest[:NX], rest[NX:]
    head = pl.program_id(0)
    slots = w_ref.shape[0] // 2
    rows = kept.shape[0]
    grad_ref[...] = jnp.zeros_like(grad_ref)

    @pl.when(head == 0)
    def _():
        codes_ref[...] = jnp.zeros_like(codes_ref)

    sides = ((q0, k0, v0, g0), (q1, k1, v1, g1))
    runs = []
    for slot in range(slots):
        for side, (q, k, v, g) in enumerate(sides):
            entry = info[1 + side * slots + slot]
            run = backward_pair(
                jnp.maximum(entry, 0),
                entry >= 0,
                q[slot],
                k[slot],
                v[slot],
                g[slot],
                w_ref[side * slots + slot],
                prompt_refs,
                blocks,
                grad_ref,
            )
            runs.append((run, (out0, out1)[side], slot))
    for time in range(len(runs) + STAGES - 1):
        for start, (run, out, slot) in enumerate(runs):
            if 0 <= time - start < STAGES:
                try:
                    next(run)
                except StopIteration as stop:
                    for index, value in enumerate(stop.value):
                        out[slot, index] = value

    kept[...] = grad_ref[:rows]
    lane = lax.broadcasted_iota(jnp.int32, (8, HD), 1)
    for index, ref in enumerate(sent):
        part = slice((index + 1) * rows, (index + 2) * rows)
        codes = codes_ref[index]
        for tile in range(4):
            value, code = to_steps(grad_ref[part, tile * HD : (tile + 1) * HD])
            ref[:, pl.ds(pl.multiple_of(head * (4 * HD) + tile * HD, HD), HD)] = value
            codes = jnp.where(lane == head * 4 + tile, code, codes)
        codes_ref[index] = codes
        ref[:, ref.shape[1] - HD :] = code_rows(codes, rows)


def chunk_backward(first, heads, place, blocks, info, queries, comp, grads, other, weights, prompt_parts):
    slots, length, width = queries.shape
    half = width // HD // 2
    rows = prompt_parts[0].shape[0]
    keys = rows * NX

    def own(offset):
        return pl.BlockSpec(
            (slots, length, HD), lambda h, info: (0, 0, offset + info[0] * half + first + h)
        )

    def sent(offset):
        return pl.BlockSpec((slots, length, HD), lambda h, info: (0, 0, offset * half + first + h))

    result = pl.BlockSpec((slots, 3, length, HD), lambda h, info: (0, 0, 0, h))
    cols = heads * 4 * HD + HD
    piece = pl.BlockSpec((rows, cols), lambda h, info: (0, 0))
    kept = pl.BlockSpec((rows, 4 * HD), lambda h, info: (0, h))
    grid_spec = pltpu.PrefetchScalarGridSpec(
        num_scalar_prefetch=1,
        grid=(heads,),
        in_specs=[
            own(0),
            own(0),
            own(2 * half),
            own(0),
            sent(0),
            sent(1),
            sent(2),
            sent(3),
            pl.BlockSpec(weights.shape, lambda h, info: (0, 0, 0)),
        ]
        + [pl.BlockSpec((rows, 4 * HD), lambda h, info: (0, place + h))] * NX,
        scratch_shapes=[pltpu.VMEM((keys, 4 * HD), F32), pltpu.VMEM((NX - 1, 8, HD), F32)],
        out_specs=[result, result, kept] + [piece] * (NX - 1),
    )
    slot_shape = jax.ShapeDtypeStruct((slots, 3, length, heads * HD), BF16)
    kept_shape = jax.ShapeDtypeStruct((rows, heads * 4 * HD), F32)
    piece_shape = jax.ShapeDtypeStruct((rows, cols), I16)
    count = heads * slots * 2
    return pl.pallas_call(
        functools.partial(chunk_kernel, blocks),
        grid_spec=grid_spec,
        out_shape=[slot_shape, slot_shape, kept_shape] + [piece_shape] * (NX - 1),
        compiler_params=pltpu.CompilerParams(
            dimension_semantics=("arbitrary",), vmem_limit_bytes=VMEM_BYTES
        ),
        cost_estimate=pl.CostEstimate(
            flops=count * 24 * (keys + length) * length * HD,
            bytes_accessed=count * 7 * length * HD * 2 + heads * keys * 4 * HD * 6,
            transcendentals=count * (keys + length) * length,
        ),
        name="head_chunk",
    )(info, queries, comp, comp, grads, other, other, other, other, weights, *prompt_parts)


def half_kernel(core_ref, *refs):
    out_ref, size = refs[-1], refs[0].shape[2]
    for index, ref in enumerate(refs[:-1]):
        out_ref[:, :, index * size : (index + 1) * size] = ref[...]


def other_half(core, queries, comp, grads):
    slots, length, width = queries.shape
    half = width // 2

    def block(first):
        return pl.BlockSpec((1, length, half), lambda s, core: (s, 0, first + 1 - core[0]))

    return pl.pallas_call(
        half_kernel,
        grid_spec=pltpu.PrefetchScalarGridSpec(
            num_scalar_prefetch=1,
            grid=(slots,),
            in_specs=[block(0), block(0), block(2), block(0)],
            out_specs=pl.BlockSpec((1, length, 4 * half), lambda s, core: (s, 0, 0)),
        ),
        out_shape=jax.ShapeDtypeStruct((slots, length, 4 * half), BF16),
        compiler_params=pltpu.CompilerParams(
            dimension_semantics=("arbitrary",), vmem_limit_bytes=MOST_BYTES
        ),
        cost_estimate=pl.CostEstimate(
            flops=0, bytes_accessed=slots * length * half * 16, transcendentals=0
        ),
        name="other_half",
    )(core[None], queries, comp, comp, grads)


def place_kernel(core_ref, *refs):
    parts, (query_out, comp_out) = refs[:-2], refs[-2:]
    count = len(parts) // 2
    half = query_out.shape[2] // 2
    core = core_ref[0]

    def fill(out):
        for side, group in ((core, parts[:count]), (1 - core, parts[count:])):
            first = 0
            for part in group:
                size = part.shape[3]
                start = pl.multiple_of(side * half + first, HD)
                out[0, :, pl.ds(start, size)] = part[0, 0]
                first += size

    @pl.when(pl.program_id(1) == 0)
    def _():
        fill(query_out)

    @pl.when(pl.program_id(1) > 0)
    def _():
        fill(comp_out)


def place_slots(core, mine, got, width):
    slots, kinds, length, _ = mine[0].shape
    total = slots * kinds * length * width * 2
    return pl.pallas_call(
        place_kernel,
        grid=(slots, kinds),
        in_specs=[pl.BlockSpec(memory_space=pltpu.SMEM)]
        + [
            pl.BlockSpec((1, 1, length, part.shape[3]), lambda s, k: (s, k, 0, 0))
            for part in (*mine, *got)
        ],
        out_specs=[
            pl.BlockSpec((1, length, width), lambda s, k: (s, 0, 0)),
            pl.BlockSpec((1, length, width), lambda s, k: (s, 0, jnp.maximum(k - 1, 0))),
        ],
        out_shape=[
            jax.ShapeDtypeStruct((slots, length, width), BF16),
            jax.ShapeDtypeStruct((slots, length, 2 * width), BF16),
        ],
        cost_estimate=pl.CostEstimate(flops=0, bytes_accessed=2 * total, transcendentals=0),
        name="place_slots",
    )(core[None], *mine, *got)


def sum_kernel(counts, coded, *refs):
    ins, outs, codes_ref = refs[: 7 * len(counts)], refs[7 * len(counts) : -1], refs[-1]
    rows = outs[0].shape[0]
    head = pl.program_id(0)
    lane = lax.broadcasted_iota(jnp.int32, (16, HD), 1)

    @pl.when(head == 0)
    def _():
        codes_ref[...] = jnp.zeros_like(codes_ref)

    def add(first, kept, arrived, codes):
        powers = [jnp.exp2(code[:16].astype(F32)) * (1.0 / STEPS) for code in codes]
        for tile in range(4):
            cols = slice(tile * HD, (tile + 1) * HD)
            total = kept[:, cols]
            here = lane == (head - first) * 4 + tile
            for ref, power in zip(arrived, powers):
                scale = jnp.sum(jnp.where(here, power, 0.0), axis=1, keepdims=True)
                total += ref[:, cols].astype(F32) * scale[:1]
            for i, out in enumerate(outs):
                value = total[i * rows : (i + 1) * rows]
                if not coded or i == 0:
                    out[:, cols] = value
                    continue
                value, code = to_steps(value)
                start = pl.multiple_of(head * (4 * HD) + tile * HD, HD)
                out[:, pl.ds(start, HD)] = value
                codes_ref[i - 1] = jnp.where(lane[:8] == head * 4 + tile, code, codes_ref[i - 1])

    first = 0
    for index, heads in enumerate(counts):
        kept, *others = ins[7 * index : 7 * index + 7]

        @pl.when((head >= first) & (head < first + heads))
        def _(first=first, kept=kept, others=others):
            add(first, kept, others[:3], others[3:])

        first += heads
    if coded:
        for i, out in enumerate(outs[1:]):
            out[:, out.shape[1] - HD :] = code_rows(codes_ref[i], rows)


def sum_parts(chunks, parts, coded):
    counts = [heads for heads, _, _ in chunks]
    total = sum(counts)
    all_rows = chunks[0][1].shape[0]
    rows, cols = all_rows // parts, total * 4 * HD
    ins, in_specs = [], []
    first = 0
    for heads, kept, arrived in chunks:
        ins += [kept, *arrived, *arrived]

        def column(h, first=first, heads=heads):
            return (0, jnp.clip(h - first, 0, heads - 1))

        def last(h, heads=heads):
            return (0, heads * 4)

        in_specs += [pl.BlockSpec((all_rows, 4 * HD), column)] * 4
        in_specs += [pl.BlockSpec((all_rows, HD), last)] * 3
        first += heads
    plain = jax.ShapeDtypeStruct((rows, cols), F32)
    out_spec = pl.BlockSpec((rows, 4 * HD), lambda h: (0, h))
    other, other_spec = plain, out_spec
    if coded:
        other = jax.ShapeDtypeStruct((rows, cols + HD), I16)
        other_spec = pl.BlockSpec((rows, cols + HD), lambda h: (0, 0))
    return pl.pallas_call(
        functools.partial(sum_kernel, counts, coded),
        grid=(total,),
        in_specs=in_specs,
        out_specs=[out_spec] + [other_spec] * (parts - 1),
        out_shape=[plain] + [other] * (parts - 1),
        scratch_shapes=[pltpu.VMEM((NX - 1, 8, HD), F32)],
        compiler_params=pltpu.CompilerParams(
            dimension_semantics=("arbitrary",), vmem_limit_bytes=SMALL_BYTES
        ),
        cost_estimate=pl.CostEstimate(
            flops=0, bytes_accessed=rows * parts * cols * 14, transcendentals=0
        ),
        name="sum_parts",
    )(*ins)


def share_kernel(core_ref, mine_ref, got_ref, out_ref):
    core_first = core_ref[0] == 0
    heads = mine_ref.shape[1] // (4 * HD)
    for head in range(heads):
        for prompt in range(2):
            for kind in range(2):
                begin = (head * 4 + prompt * 2 + kind) * HD
                mine, got = mine_ref[:, begin : begin + HD], got_ref[:, begin : begin + HD]
                low, high = jnp.where(core_first, mine, got), jnp.where(core_first, got, mine)
                for side, value in enumerate((low, high)):
                    start = ((kind * 2 + side) * heads + head) * HD
                    out_ref[:, prompt, start : start + HD] = value


def place_share(core, mine, got):
    rows, width = mine.shape
    vmem = pl.BlockSpec(memory_space=pltpu.VMEM)
    return pl.pallas_call(
        share_kernel,
        in_specs=[pl.BlockSpec(memory_space=pltpu.SMEM), vmem, vmem],
        out_specs=vmem,
        out_shape=jax.ShapeDtypeStruct((rows, 2, width), F32),
        name="place_share",
    )(core[None], mine, got)


def three_parts(value):
    parts = []
    for _ in range(3):
        part = lax.reduce_precision(value, 8, 7)
        parts.append(part.astype(BF16))
        value = value - part
    return parts


def per_device(
    prompt_kv, queries, completion_kv, out_grad, rewards, token_mask, sample_lists, prompt_samples
):
    myself = lax.axis_index("samp")
    core = lax.rem(myself, 2)
    prompt_kv, queries, comp, grads = prompt_kv[0], queries[0], completion_kv[0], out_grad[0]
    slots, length, width = queries.shape
    half_width = width // 2
    half_heads = half_width // HD
    own_rows, prompts = prompt_kv.shape[0], prompt_kv.shape[1]

    lists_all = sample_lists[0]
    my_list = lax.dynamic_index_in_dim(lists_all, myself, 0, keepdims=False)
    lists = jnp.concatenate(
        [my_list, lax.dynamic_index_in_dim(lists_all, myself + 1 - 2 * core, 0, keepdims=False)]
    )
    live = (lists >= 0).astype(F32)
    member = (lists[:, None] == jnp.arange(prompts, dtype=jnp.int32)[None, :]).astype(F32)
    my_masks = token_mask[0].astype(F32)
    counts = jnp.stack(
        [jnp.sum(jnp.sum(my_masks, axis=1) * live[:slots]), jnp.sum(live[:slots])]
    )
    counts = sum_axis(jnp.broadcast_to(jnp.pad(counts, (0, 6))[:, None], (8, HD)), "dp")[:2, 0]
    my_stats = jnp.concatenate([jnp.sum(member[:slots] * rewards[0][:, None], axis=0), counts])

    facts = jnp.concatenate([my_masks, jnp.broadcast_to(rewards[0][:, None], (slots, length))], axis=0)
    facts_other = jnp.concatenate(
        [facts, jnp.pad(my_stats, (0, length - my_stats.shape[0]))[None, :]], axis=0
    )
    facts_other = move_core(facts_other)
    masks = jnp.concatenate([my_masks, facts_other[:slots]], axis=0)
    reward = jnp.concatenate([facts[slots:, 0], facts_other[slots : 2 * slots, 0]])
    stats = my_stats + facts_other[2 * slots, : prompts + 2]
    stats = jnp.concatenate(three_parts(stats))
    stats = jnp.pad(stats[None, :], ((0, 2 * own_rows - 1), (0, HD - stats.shape[0])))

    kv_heads = prompt_kv.reshape(own_rows, prompts, 2, 2, half_heads, HD)
    kv_heads = jnp.transpose(kv_heads, (3, 0, 4, 1, 2, 5)).reshape(2, own_rows, -1)
    kv_mine = lax.dynamic_index_in_dim(kv_heads, core, 0, keepdims=False)
    kv_sent = lax.dynamic_index_in_dim(kv_heads, 1 - core, 0, keepdims=False)
    kv_other = move_core(kv_sent)

    block = jnp.concatenate([kv_mine, kv_other], axis=0)

    edge = CHUNKS[0] * 4 * HD
    early = jnp.concatenate([block[:, :edge], stats], axis=1)
    near = gather_axis(early, "y")
    beside = gather_axis(block[:, edge:], "x")

    later_core, near, beside = lax.optimization_barrier((core, near, beside))
    other = move_core(other_half(later_core, queries, comp, grads))
    late = jnp.concatenate(beside, axis=0)

    early = gather_axis(jnp.concatenate(near, axis=0), "x")
    stats = jnp.sum(sum(value[:, edge:].astype(F32) for value in early), axis=0)
    stats = jnp.sum(stats[: 3 * (prompts + 2)].reshape(3, prompts + 2), axis=0)
    reward_mean = stats[:prompts] / prompt_samples[0].astype(F32)
    advantage = reward - jnp.sum(member * reward_mean[None, :], axis=1)
    factor = length * stats[prompts + 1] / stats[prompts]
    weights = masks * advantage[:, None] * factor
    weights = jnp.broadcast_to(weights[:, :, None], (2 * slots, length, HD))

    info = jnp.concatenate([core[None], lists]).astype(jnp.int32)
    info, late = lax.optimization_barrier((info, late))
    late = gather_axis(late, "y")
    straight = list(range(BLOCKS))
    turned = [i * NX + j for j in range(NX) for i in range(NY)]
    mine_parts, other_parts, waiting = [], [], []
    first = 0
    for heads in CHUNKS:
        early_chunk = first == 0
        outs = chunk_backward(
            first,
            heads,
            0 if early_chunk else first - CHUNKS[0],
            straight if early_chunk else turned,
            info,
            queries,
            comp,
            grads,
            other,
            weights,
            early if early_chunk else late,
        )
        first += heads
        mine, theirs, kept, *sent = outs
        if early_chunk:
            late, kept, sent, theirs = lax.optimization_barrier((late, kept, sent, theirs))
        else:
            count, *arrived = waiting.pop()
            arrived, moved, kept, sent, theirs = lax.optimization_barrier(
                (arrived, other_parts.pop(), kept, sent, theirs)
            )
            other_parts.append(moved)
            waiting.append((count, *arrived))
        info, _ = lax.optimization_barrier((info, kept))
        mine_parts.append(mine)
        arrived = [move_axis(value, "x", -step) for step, value in enumerate(sent, 1)]
        waiting.append((heads, kept, arrived))
        other_parts.append(move_core(theirs))

    query_out, comp_out = place_slots(core, mine_parts, other_parts, width)
    count, kept, arrived = waiting.pop()
    line = sum_parts(waiting, NY, True)
    near = [move_axis(line[step], "y", -step) for step in (1, 3)]
    arrived, near, far, query_out, comp_out = lax.optimization_barrier(
        (arrived, near, line[2], query_out, comp_out)
    )
    back = [near[0], move_axis(far, "y", -2), near[1]]
    last = sum_parts([(count, kept, arrived)], NY, True)
    last_back = [move_axis(last[step], "y", -step) for step in (1, 2, 3)]
    ends = [(half_heads - count, line[0], back), (count, last[0], last_back)]
    mine, theirs = sum_parts(ends, 2, False)
    share = place_share(core, mine, move_core(theirs))
    return (query_out[None], comp_out[None], share[None])


def solution(mesh):
    in_specs = (
        P("dp", "samp", None, None),
        P("dp", "samp", None, None),
        P("dp", "samp", None, None),
        P("dp", "samp", None, None),
        P("dp", "samp"),
        P("dp", "samp", None),
        P("dp", None, None),
        P("dp", None),
    )
    out_specs = (
        P("dp", "samp", None, None),
        P("dp", "samp", None, None),
        P("dp", "samp", None, None),
    )
    return jax.shard_map(
        per_device, mesh=mesh, in_specs=in_specs, out_specs=out_specs, check_vma=False
    )
```

```python
import functools
import math

import jax
import jax.numpy as jnp
from jax import lax
from jax.experimental import pallas as pl
from jax.experimental.pallas import tpu as pltpu
from jax.sharding import PartitionSpec as P

HD = 128
NX, NY, NC = 4, 4, 2
CHUNKS = (3, 3, 2)
BLOCKS = NX * NY
STEPS = 32760.0
STAGES = 5
VMEM_BYTES = 48 * 1024 * 1024
SMALL_BYTES = 32 * 1024 * 1024
MOST_BYTES = 60 * 1024 * 1024
F32 = jnp.float32
BF16 = jnp.bfloat16
I16 = jnp.int16


def shift_pairs(dx, dy, dc):
    pairs = []
    for x in range(NX):
        for y in range(NY):
            for c in range(NC):
                to_x, to_y, to_c = (x + dx) % NX, (y + dy) % NY, (c + dc) % NC
                pairs.append(((x * NY + y) * NC + c, (to_x * NY + to_y) * NC + to_c))
    return pairs


def move_core(value):
    return lax.ppermute(value, "samp", shift_pairs(0, 0, 1))


def move_axis(value, axis, step):
    if axis == "x":
        return lax.ppermute(value, "samp", shift_pairs(step, 0, 0))
    if axis == "y":
        return lax.ppermute(value, "samp", shift_pairs(0, step, 0))
    return lax.ppermute(value, "dp", [(i, (i + step) % 4) for i in range(4)])


def gather_axis(value, axis):
    return [value] + [move_axis(value, axis, step) for step in (1, 2, 3)]


def sum_axis(value, axis):
    first, second, third, fourth = gather_axis(value, axis)
    return (first + second) + (third + fourth)


def to_steps(value):
    peak = jnp.max(jnp.max(jnp.abs(value), axis=0, keepdims=True), axis=1, keepdims=True)
    code = jnp.floor(jnp.log2(jnp.clip(peak, 1e-30, 1e30))) + 1.0
    steps = jnp.floor(value * (jnp.exp2(-code) * STEPS) + 0.5)
    return steps.astype(jnp.int32).astype(I16), code


def code_rows(codes, rows):
    return jnp.broadcast_to(codes[:1], (rows, HD)).astype(jnp.int32).astype(I16)


def backward_pair(prompt, live, query, comp_k, comp_v, grad, weight, prompt_refs, blocks, grad_ref):
    scale = HD**-0.5
    base2 = scale * math.log2(math.e)
    nt = (((1,), (1,)), ((), ()))
    tn = (((0,), (0,)), ((), ()))
    nn = (((1,), (0,)), ((), ()))

    def dot(a, b, dims):
        return lax.dot_general(a, b, dims, preferred_element_type=F32)

    key_col = pl.multiple_of(prompt * (2 * HD), 2 * HD)
    val_col = pl.multiple_of(prompt * (2 * HD) + HD, HD)
    size = prompt_refs[0].shape[0] * len(prompt_refs) // BLOCKS

    def prompt_rows(col):
        parts = []
        for block in blocks:
            ref, place = prompt_refs[block // NX], block % NX
            parts.append(ref[place * size : (place + 1) * size, pl.ds(col, HD)])
        return jnp.concatenate(parts, axis=0)

    prompt_k, prompt_v = prompt_rows(key_col), prompt_rows(val_col)
    query = jnp.where(live, query, jnp.zeros_like(query))
    weighted = (grad.astype(F32) * weight).astype(BF16)
    weighted = jnp.where(live, weighted, jnp.zeros_like(weighted))

    s_p = dot(prompt_k, query, nt)
    s_c = dot(comp_k, query, nt)
    yield
    peak = jnp.maximum(jnp.max(s_p, axis=0, keepdims=True), jnp.max(s_c, axis=0, keepdims=True))
    peak = peak * base2
    e_p = jnp.exp2(s_p * base2 - peak)
    e_c = jnp.exp2(s_c * base2 - peak)
    total = jnp.sum(e_p, axis=0, keepdims=True) + jnp.sum(e_c, axis=0, keepdims=True)
    inverse = 1.0 / total
    p_p = e_p * inverse
    p_c = e_c * inverse
    low_p = p_p.astype(BF16)
    low_c = p_c.astype(BF16)
    yield
    d_p = dot(prompt_v, weighted, nt)
    d_c = dot(comp_v, weighted, nt)
    row_dot = jnp.sum(low_p.astype(F32) * d_p, axis=0, keepdims=True) + jnp.sum(
        low_c.astype(F32) * d_c, axis=0, keepdims=True
    )
    yield
    ds_p = (p_p * (d_p - row_dot)).astype(BF16)
    ds_c = (p_c * (d_c - row_dot)).astype(BF16)
    yield
    dv_p = dot(low_p, weighted, nn)
    dk_p = dot(ds_p, query, nn) * scale
    grad_ref[:, pl.ds(key_col, HD)] += dk_p
    grad_ref[:, pl.ds(val_col, HD)] += dv_p
    dk_c = (dot(ds_c, query, nn) * scale).astype(BF16)
    dv_c = dot(low_c, weighted, nn).astype(BF16)
    dq = ((dot(prompt_k, ds_p, tn) + dot(comp_k, ds_c, tn)) * scale).T.astype(BF16)
    return dq, dk_c, dv_c


def chunk_kernel(
    blocks, info, q0, k0, v0, g0, q1, k1, v1, g1, w_ref, *rest
):
    prompt_refs, (out0, out1, kept, *sent, grad_ref, codes_ref) = rest[:NX], rest[NX:]
    head = pl.program_id(0)
    slots = w_ref.shape[0] // 2
    rows = kept.shape[0]
    grad_ref[...] = jnp.zeros_like(grad_ref)

    @pl.when(head == 0)
    def _():
        codes_ref[...] = jnp.zeros_like(codes_ref)

    sides = ((q0, k0, v0, g0), (q1, k1, v1, g1))
    runs = []
    for slot in range(slots):
        for side, (q, k, v, g) in enumerate(sides):
            entry = info[1 + side * slots + slot]
            run = backward_pair(
                jnp.maximum(entry, 0),
                entry >= 0,
                q[slot],
                k[slot],
                v[slot],
                g[slot],
                w_ref[side * slots + slot],
                prompt_refs,
                blocks,
                grad_ref,
            )
            runs.append((run, (out0, out1)[side], slot))
    for time in range(len(runs) + STAGES - 1):
        for start, (run, out, slot) in enumerate(runs):
            if 0 <= time - start < STAGES:
                try:
                    next(run)
                except StopIteration as stop:
                    for index, value in enumerate(stop.value):
                        out[slot, index] = value

    kept[...] = grad_ref[:rows]
    lane = lax.broadcasted_iota(jnp.int32, (8, HD), 1)
    for index, ref in enumerate(sent):
        part = slice((index + 1) * rows, (index + 2) * rows)
        codes = codes_ref[index]
        for tile in range(4):
            value, code = to_steps(grad_ref[part, tile * HD : (tile + 1) * HD])
            ref[:, pl.ds(pl.multiple_of(head * (4 * HD) + tile * HD, HD), HD)] = value
            codes = jnp.where(lane == head * 4 + tile, code, codes)
        codes_ref[index] = codes
        ref[:, ref.shape[1] - HD :] = code_rows(codes, rows)


def chunk_backward(first, heads, place, blocks, info, queries, comp, grads, other, weights, prompt_parts):
    slots, length, width = queries.shape
    half = width // HD // 2
    rows = prompt_parts[0].shape[0]
    keys = rows * NX

    def own(offset):
        return pl.BlockSpec(
            (slots, length, HD), lambda h, info: (0, 0, offset + info[0] * half + first + h)
        )

    def sent(offset):
        return pl.BlockSpec((slots, length, HD), lambda h, info: (0, 0, offset * half + first + h))

    result = pl.BlockSpec((slots, 3, length, HD), lambda h, info: (0, 0, 0, h))
    cols = heads * 4 * HD + HD
    piece = pl.BlockSpec((rows, cols), lambda h, info: (0, 0))
    kept = pl.BlockSpec((rows, 4 * HD), lambda h, info: (0, h))
    grid_spec = pltpu.PrefetchScalarGridSpec(
        num_scalar_prefetch=1,
        grid=(heads,),
        in_specs=[
            own(0),
            own(0),
            own(2 * half),
            own(0),
            sent(0),
            sent(1),
            sent(2),
            sent(3),
            pl.BlockSpec(weights.shape, lambda h, info: (0, 0, 0)),
        ]
        + [pl.BlockSpec((rows, 4 * HD), lambda h, info: (0, place + h))] * NX,
        scratch_shapes=[pltpu.VMEM((keys, 4 * HD), F32), pltpu.VMEM((NX - 1, 8, HD), F32)],
        out_specs=[result, result, kept] + [piece] * (NX - 1),
    )
    slot_shape = jax.ShapeDtypeStruct((slots, 3, length, heads * HD), BF16)
    kept_shape = jax.ShapeDtypeStruct((rows, heads * 4 * HD), F32)
    piece_shape = jax.ShapeDtypeStruct((rows, cols), I16)
    count = heads * slots * 2
    return pl.pallas_call(
        functools.partial(chunk_kernel, blocks),
        grid_spec=grid_spec,
        out_shape=[slot_shape, slot_shape, kept_shape] + [piece_shape] * (NX - 1),
        compiler_params=pltpu.CompilerParams(
            dimension_semantics=("arbitrary",), vmem_limit_bytes=VMEM_BYTES
        ),
        cost_estimate=pl.CostEstimate(
            flops=count * 24 * (keys + length) * length * HD,
            bytes_accessed=count * 7 * length * HD * 2 + heads * keys * 4 * HD * 6,
            transcendentals=count * (keys + length) * length,
        ),
        name="head_chunk",
    )(info, queries, comp, comp, grads, other, other, other, other, weights, *prompt_parts)


def half_kernel(core_ref, *refs):
    out_ref, size = refs[-1], refs[0].shape[2]
    for index, ref in enumerate(refs[:-1]):
        out_ref[:, :, index * size : (index + 1) * size] = ref[...]


def other_half(core, queries, comp, grads):
    slots, length, width = queries.shape
    half = width // 2

    def block(first):
        return pl.BlockSpec((1, length, half), lambda s, core: (s, 0, first + 1 - core[0]))

    return pl.pallas_call(
        half_kernel,
        grid_spec=pltpu.PrefetchScalarGridSpec(
            num_scalar_prefetch=1,
            grid=(slots,),
            in_specs=[block(0), block(0), block(2), block(0)],
            out_specs=pl.BlockSpec((1, length, 4 * half), lambda s, core: (s, 0, 0)),
        ),
        out_shape=jax.ShapeDtypeStruct((slots, length, 4 * half), BF16),
        compiler_params=pltpu.CompilerParams(
            dimension_semantics=("arbitrary",), vmem_limit_bytes=MOST_BYTES
        ),
        cost_estimate=pl.CostEstimate(
            flops=0, bytes_accessed=slots * length * half * 16, transcendentals=0
        ),
        name="other_half",
    )(core[None], queries, comp, comp, grads)


def place_kernel(core_ref, *refs):
    parts, (query_out, comp_out) = refs[:-2], refs[-2:]
    count = len(parts) // 2
    half = query_out.shape[2] // 2
    core = core_ref[0]

    def fill(out):
        for side, group in ((core, parts[:count]), (1 - core, parts[count:])):
            first = 0
            for part in group:
                size = part.shape[3]
                start = pl.multiple_of(side * half + first, HD)
                out[0, :, pl.ds(start, size)] = part[0, 0]
                first += size

    @pl.when(pl.program_id(1) == 0)
    def _():
        fill(query_out)

    @pl.when(pl.program_id(1) > 0)
    def _():
        fill(comp_out)


def place_slots(core, mine, got, width):
    slots, kinds, length, _ = mine[0].shape
    total = slots * kinds * length * width * 2
    return pl.pallas_call(
        place_kernel,
        grid=(slots, kinds),
        in_specs=[pl.BlockSpec(memory_space=pltpu.SMEM)]
        + [
            pl.BlockSpec((1, 1, length, part.shape[3]), lambda s, k: (s, k, 0, 0))
            for part in (*mine, *got)
        ],
        out_specs=[
            pl.BlockSpec((1, length, width), lambda s, k: (s, 0, 0)),
            pl.BlockSpec((1, length, width), lambda s, k: (s, 0, jnp.maximum(k - 1, 0))),
        ],
        out_shape=[
            jax.ShapeDtypeStruct((slots, length, width), BF16),
            jax.ShapeDtypeStruct((slots, length, 2 * width), BF16),
        ],
        cost_estimate=pl.CostEstimate(flops=0, bytes_accessed=2 * total, transcendentals=0),
        name="place_slots",
    )(core[None], *mine, *got)


def place_last_kernel(core_ref, query_in, comp_in, mine_ref, got_ref, query_out, comp_out):
    del core_ref, query_in, comp_in
    side, kind = pl.program_id(0), pl.program_id(1)
    for place, source in enumerate((mine_ref, got_ref)):

        @pl.when((side == place) & (kind == 0))
        def _(source=source):
            query_out[...] = source[:, 0]

        @pl.when((side == place) & (kind > 0))
        def _(source=source):
            comp_out[...] = source[:, 0]


def place_last(core, query_out, comp_out, mine, got):
    slots, kinds, length, size = mine.shape
    width = query_out.shape[2]
    count = width // 2 // size
    anywhere = pl.BlockSpec(memory_space=pl.ANY)
    part = pl.BlockSpec((slots, 1, length, size), lambda d, k, core: (0, k, 0, 0))

    def column(d, core):
        return (core[0] + d - 2 * d * core[0]) * count + count - 1

    return pl.pallas_call(
        place_last_kernel,
        grid_spec=pltpu.PrefetchScalarGridSpec(
            num_scalar_prefetch=1,
            grid=(2, kinds),
            in_specs=[anywhere, anywhere, part, part],
            out_specs=[
                pl.BlockSpec((slots, length, size), lambda d, k, core: (0, 0, column(d, core))),
                pl.BlockSpec(
                    (slots, length, size),
                    lambda d, k, core: (0, 0, jnp.maximum(k - 1, 0) * 2 * count + column(d, core)),
                ),
            ],
        ),
        out_shape=[
            jax.ShapeDtypeStruct(query_out.shape, BF16),
            jax.ShapeDtypeStruct(comp_out.shape, BF16),
        ],
        input_output_aliases={1: 0, 2: 1},
        compiler_params=pltpu.CompilerParams(
            dimension_semantics=("arbitrary", "arbitrary"), vmem_limit_bytes=SMALL_BYTES
        ),
        cost_estimate=pl.CostEstimate(
            flops=0, bytes_accessed=8 * slots * kinds * length * size, transcendentals=0
        ),
        name="place_last",
    )(core[None], query_out, comp_out, mine, got)


def sum_kernel(counts, coded, *refs):
    ins, outs, codes_ref = refs[: 7 * len(counts)], refs[7 * len(counts) : -1], refs[-1]
    rows = outs[0].shape[0]
    head = pl.program_id(0)
    lane = lax.broadcasted_iota(jnp.int32, (16, HD), 1)

    @pl.when(head == 0)
    def _():
        codes_ref[...] = jnp.zeros_like(codes_ref)

    def add(first, kept, arrived, codes):
        powers = [jnp.exp2(code[:16].astype(F32)) * (1.0 / STEPS) for code in codes]
        for tile in range(4):
            cols = slice(tile * HD, (tile + 1) * HD)
            total = kept[:, cols]
            here = lane == (head - first) * 4 + tile
            for ref, power in zip(arrived, powers):
                scale = jnp.sum(jnp.where(here, power, 0.0), axis=1, keepdims=True)
                total += ref[:, cols].astype(F32) * scale[:1]
            for i, out in enumerate(outs):
                value = total[i * rows : (i + 1) * rows]
                if not coded or i == 0:
                    out[:, cols] = value
                    continue
                value, code = to_steps(value)
                start = pl.multiple_of(head * (4 * HD) + tile * HD, HD)
                out[:, pl.ds(start, HD)] = value
                codes_ref[i - 1] = jnp.where(lane[:8] == head * 4 + tile, code, codes_ref[i - 1])

    first = 0
    for index, heads in enumerate(counts):
        kept, *others = ins[7 * index : 7 * index + 7]

        @pl.when((head >= first) & (head < first + heads))
        def _(first=first, kept=kept, others=others):
            add(first, kept, others[:3], others[3:])

        first += heads
    if coded:
        for i, out in enumerate(outs[1:]):
            out[:, out.shape[1] - HD :] = code_rows(codes_ref[i], rows)


def sum_parts(chunks, parts, coded):
    counts = [heads for heads, _, _ in chunks]
    total = sum(counts)
    all_rows = chunks[0][1].shape[0]
    rows, cols = all_rows // parts, total * 4 * HD
    ins, in_specs = [], []
    first = 0
    for heads, kept, arrived in chunks:
        ins += [kept, *arrived, *arrived]

        def column(h, first=first, heads=heads):
            return (0, jnp.clip(h - first, 0, heads - 1))

        def last(h, heads=heads):
            return (0, heads * 4)

        in_specs += [pl.BlockSpec((all_rows, 4 * HD), column)] * 4
        in_specs += [pl.BlockSpec((all_rows, HD), last)] * 3
        first += heads
    plain = jax.ShapeDtypeStruct((rows, cols), F32)
    out_spec = pl.BlockSpec((rows, 4 * HD), lambda h: (0, h))
    other, other_spec = plain, out_spec
    if coded:
        other = jax.ShapeDtypeStruct((rows, cols + HD), I16)
        other_spec = pl.BlockSpec((rows, cols + HD), lambda h: (0, 0))
    return pl.pallas_call(
        functools.partial(sum_kernel, counts, coded),
        grid=(total,),
        in_specs=in_specs,
        out_specs=[out_spec] + [other_spec] * (parts - 1),
        out_shape=[plain] + [other] * (parts - 1),
        scratch_shapes=[pltpu.VMEM((NX - 1, 8, HD), F32)],
        compiler_params=pltpu.CompilerParams(
            dimension_semantics=("arbitrary",), vmem_limit_bytes=SMALL_BYTES
        ),
        cost_estimate=pl.CostEstimate(
            flops=0, bytes_accessed=rows * parts * cols * 14, transcendentals=0
        ),
        name="sum_parts",
    )(*ins)


def share_kernel(core_ref, mine_ref, got_ref, out_ref):
    core_first = core_ref[0] == 0
    heads = mine_ref.shape[1] // (4 * HD)
    for head in range(heads):
        for prompt in range(2):
            for kind in range(2):
                begin = (head * 4 + prompt * 2 + kind) * HD
                mine, got = mine_ref[:, begin : begin + HD], got_ref[:, begin : begin + HD]
                low, high = jnp.where(core_first, mine, got), jnp.where(core_first, got, mine)
                for side, value in enumerate((low, high)):
                    start = ((kind * 2 + side) * heads + head) * HD
                    out_ref[:, prompt, start : start + HD] = value


def place_share(core, mine, got):
    rows, width = mine.shape
    vmem = pl.BlockSpec(memory_space=pltpu.VMEM)
    return pl.pallas_call(
        share_kernel,
        in_specs=[pl.BlockSpec(memory_space=pltpu.SMEM), vmem, vmem],
        out_specs=vmem,
        out_shape=jax.ShapeDtypeStruct((rows, 2, width), F32),
        name="place_share",
    )(core[None], mine, got)


def three_parts(value):
    parts = []
    for _ in range(3):
        part = lax.reduce_precision(value, 8, 7)
        parts.append(part.astype(BF16))
        value = value - part
    return parts


def per_device(
    prompt_kv, queries, completion_kv, out_grad, rewards, token_mask, sample_lists, prompt_samples
):
    myself = lax.axis_index("samp")
    core = lax.rem(myself, 2)
    prompt_kv, queries, comp, grads = prompt_kv[0], queries[0], completion_kv[0], out_grad[0]
    slots, length, width = queries.shape
    half_width = width // 2
    half_heads = half_width // HD
    own_rows, prompts = prompt_kv.shape[0], prompt_kv.shape[1]

    lists_all = sample_lists[0]
    my_list = lax.dynamic_index_in_dim(lists_all, myself, 0, keepdims=False)
    lists = jnp.concatenate(
        [my_list, lax.dynamic_index_in_dim(lists_all, myself + 1 - 2 * core, 0, keepdims=False)]
    )
    live = (lists >= 0).astype(F32)
    member = (lists[:, None] == jnp.arange(prompts, dtype=jnp.int32)[None, :]).astype(F32)
    my_masks = token_mask[0].astype(F32)
    counts = jnp.stack(
        [jnp.sum(jnp.sum(my_masks, axis=1) * live[:slots]), jnp.sum(live[:slots])]
    )
    counts = sum_axis(jnp.broadcast_to(jnp.pad(counts, (0, 6))[:, None], (8, HD)), "dp")[:2, 0]
    my_stats = jnp.concatenate([jnp.sum(member[:slots] * rewards[0][:, None], axis=0), counts])

    facts = jnp.concatenate([my_masks, jnp.broadcast_to(rewards[0][:, None], (slots, length))], axis=0)
    facts_other = jnp.concatenate(
        [facts, jnp.pad(my_stats, (0, length - my_stats.shape[0]))[None, :]], axis=0
    )
    facts_other = move_core(facts_other)
    masks = jnp.concatenate([my_masks, facts_other[:slots]], axis=0)
    reward = jnp.concatenate([facts[slots:, 0], facts_other[slots : 2 * slots, 0]])
    stats = my_stats + facts_other[2 * slots, : prompts + 2]
    stats = jnp.concatenate(three_parts(stats))
    stats = jnp.pad(stats[None, :], ((0, 2 * own_rows - 1), (0, HD - stats.shape[0])))

    kv_heads = prompt_kv.reshape(own_rows, prompts, 2, 2, half_heads, HD)
    kv_heads = jnp.transpose(kv_heads, (3, 0, 4, 1, 2, 5)).reshape(2, own_rows, -1)
    kv_mine = lax.dynamic_index_in_dim(kv_heads, core, 0, keepdims=False)
    kv_sent = lax.dynamic_index_in_dim(kv_heads, 1 - core, 0, keepdims=False)
    kv_other = move_core(kv_sent)

    block = jnp.concatenate([kv_mine, kv_other], axis=0)

    edge = CHUNKS[0] * 4 * HD
    early = jnp.concatenate([block[:, :edge], stats], axis=1)
    near = gather_axis(early, "y")
    beside = gather_axis(block[:, edge:], "x")

    other = other_half(core, queries, comp, grads)
    other, near, beside = lax.optimization_barrier((other, near, beside))
    other = move_core(other)
    late = jnp.concatenate(beside, axis=0)

    early = gather_axis(jnp.concatenate(near, axis=0), "x")
    stats = jnp.sum(sum(value[:, edge:].astype(F32) for value in early), axis=0)
    stats = jnp.sum(stats[: 3 * (prompts + 2)].reshape(3, prompts + 2), axis=0)
    reward_mean = stats[:prompts] / prompt_samples[0].astype(F32)
    advantage = reward - jnp.sum(member * reward_mean[None, :], axis=1)
    factor = length * stats[prompts + 1] / stats[prompts]
    weights = masks * advantage[:, None] * factor
    weights = jnp.broadcast_to(weights[:, :, None], (2 * slots, length, HD))

    info = jnp.concatenate([core[None], lists]).astype(jnp.int32)
    info, late = lax.optimization_barrier((info, late))
    late = gather_axis(late, "y")
    straight = list(range(BLOCKS))
    turned = [i * NX + j for j in range(NX) for i in range(NY)]
    mine_parts, other_parts, waiting = [], [], []
    first = 0
    for heads in CHUNKS:
        early_chunk = first == 0
        outs = chunk_backward(
            first,
            heads,
            0 if early_chunk else first - CHUNKS[0],
            straight if early_chunk else turned,
            info,
            queries,
            comp,
            grads,
            other,
            weights,
            early if early_chunk else late,
        )
        first += heads
        mine, theirs, kept, *sent = outs
        if early_chunk:
            late, kept, sent, theirs = lax.optimization_barrier((late, kept, sent, theirs))
        else:
            count, *arrived = waiting.pop()
            if first == half_heads:
                later_core, moved, kept = lax.optimization_barrier((core, other_parts.pop(), kept))
                other_parts.append(moved)
                query_out, comp_out = place_slots(later_core, mine_parts, other_parts, width)
                arrived, query_out, comp_out = lax.optimization_barrier(
                    (arrived, query_out, comp_out)
                )
            arrived, moved, kept, sent, theirs = lax.optimization_barrier(
                (arrived, other_parts.pop(), kept, sent, theirs)
            )
            other_parts.append(moved)
            waiting.append((count, *arrived))
        info, _ = lax.optimization_barrier((info, kept))
        mine_parts.append(mine)
        arrived = [move_axis(value, "x", -step) for step, value in enumerate(sent, 1)]
        waiting.append((heads, kept, arrived))
        other_parts.append(move_core(theirs))

    query_out, comp_out = place_last(
        core, query_out, comp_out, mine_parts[-1], other_parts[-1]
    )
    count, kept, arrived = waiting.pop()
    line = sum_parts(waiting, NY, True)
    near = [move_axis(line[step], "y", -step) for step in (1, 3)]
    arrived, near, far, query_out, comp_out = lax.optimization_barrier(
        (arrived, near, line[2], query_out, comp_out)
    )
    back = [near[0], move_axis(far, "y", -2), near[1]]
    last = sum_parts([(count, kept, arrived)], NY, True)
    last_back = [move_axis(last[step], "y", -step) for step in (1, 2, 3)]
    ends = [(half_heads - count, line[0], back), (count, last[0], last_back)]
    mine, theirs = sum_parts(ends, 2, False)
    share = place_share(core, mine, move_core(theirs))
    return (query_out[None], comp_out[None], share[None])


def solution(mesh):
    in_specs = (
        P("dp", "samp", None, None),
        P("dp", "samp", None, None),
        P("dp", "samp", None, None),
        P("dp", "samp", None, None),
        P("dp", "samp"),
        P("dp", "samp", None),
        P("dp", None, None),
        P("dp", None),
    )
    out_specs = (
        P("dp", "samp", None, None),
        P("dp", "samp", None, None),
        P("dp", "samp", None, None),
    )
    return jax.shard_map(
        per_device, mesh=mesh, in_specs=in_specs, out_specs=out_specs, check_vma=False
    )
```

```python
import functools
import math

import jax
import jax.numpy as jnp
from jax import lax
from jax.experimental import pallas as pl
from jax.experimental.pallas import tpu as pltpu
from jax.sharding import PartitionSpec as P

HD = 128
NX, NY, NC = 4, 4, 2
CHUNKS = (3, 3, 2)
BLOCKS = NX * NY
STEPS = 32760.0
STAGES = 5
VMEM_BYTES = 48 * 1024 * 1024
SMALL_BYTES = 32 * 1024 * 1024
MOST_BYTES = 60 * 1024 * 1024
F32 = jnp.float32
BF16 = jnp.bfloat16
I16 = jnp.int16


def shift_pairs(dx, dy, dc):
    pairs = []
    for x in range(NX):
        for y in range(NY):
            for c in range(NC):
                to_x, to_y, to_c = (x + dx) % NX, (y + dy) % NY, (c + dc) % NC
                pairs.append(((x * NY + y) * NC + c, (to_x * NY + to_y) * NC + to_c))
    return pairs


def move_core(value):
    return lax.ppermute(value, "samp", shift_pairs(0, 0, 1))


def move_axis(value, axis, step):
    if axis == "x":
        return lax.ppermute(value, "samp", shift_pairs(step, 0, 0))
    if axis == "y":
        return lax.ppermute(value, "samp", shift_pairs(0, step, 0))
    return lax.ppermute(value, "dp", [(i, (i + step) % 4) for i in range(4)])


def gather_axis(value, axis):
    return [value] + [move_axis(value, axis, step) for step in (1, 2, 3)]


def sum_axis(value, axis):
    first, second, third, fourth = gather_axis(value, axis)
    return (first + second) + (third + fourth)


def to_steps(value):
    peak = jnp.max(jnp.max(jnp.abs(value), axis=0, keepdims=True), axis=1, keepdims=True)
    code = jnp.floor(jnp.log2(jnp.clip(peak, 1e-30, 1e30))) + 1.0
    steps = jnp.floor(value * (jnp.exp2(-code) * STEPS) + 0.5)
    return steps.astype(jnp.int32).astype(I16), code


def code_rows(codes, rows):
    return jnp.broadcast_to(codes[:1], (rows, HD)).astype(jnp.int32).astype(I16)


def backward_pair(prompt, live, query, comp_k, comp_v, grad, weight, prompt_refs, blocks, grad_ref):
    scale = HD**-0.5
    base2 = scale * math.log2(math.e)
    nt = (((1,), (1,)), ((), ()))
    tn = (((0,), (0,)), ((), ()))
    nn = (((1,), (0,)), ((), ()))

    def dot(a, b, dims):
        return lax.dot_general(a, b, dims, preferred_element_type=F32)

    key_col = pl.multiple_of(prompt * (2 * HD), 2 * HD)
    val_col = pl.multiple_of(prompt * (2 * HD) + HD, HD)
    size = prompt_refs[0].shape[0] * len(prompt_refs) // BLOCKS

    def prompt_rows(col):
        parts = []
        for block in blocks:
            ref, place = prompt_refs[block // NX], block % NX
            parts.append(ref[place * size : (place + 1) * size, pl.ds(col, HD)])
        return jnp.concatenate(parts, axis=0)

    prompt_k, prompt_v = prompt_rows(key_col), prompt_rows(val_col)
    query = jnp.where(live, query, jnp.zeros_like(query))
    weighted = (grad.astype(F32) * weight).astype(BF16)
    weighted = jnp.where(live, weighted, jnp.zeros_like(weighted))

    s_p = dot(prompt_k, query, nt)
    s_c = dot(comp_k, query, nt)
    yield
    peak = jnp.maximum(jnp.max(s_p, axis=0, keepdims=True), jnp.max(s_c, axis=0, keepdims=True))
    peak = peak * base2
    e_p = jnp.exp2(s_p * base2 - peak)
    e_c = jnp.exp2(s_c * base2 - peak)
    total = jnp.sum(e_p, axis=0, keepdims=True) + jnp.sum(e_c, axis=0, keepdims=True)
    inverse = 1.0 / total
    p_p = e_p * inverse
    p_c = e_c * inverse
    low_p = p_p.astype(BF16)
    low_c = p_c.astype(BF16)
    yield
    d_p = dot(prompt_v, weighted, nt)
    d_c = dot(comp_v, weighted, nt)
    row_dot = jnp.sum(low_p.astype(F32) * d_p, axis=0, keepdims=True) + jnp.sum(
        low_c.astype(F32) * d_c, axis=0, keepdims=True
    )
    yield
    ds_p = (p_p * (d_p - row_dot)).astype(BF16)
    ds_c = (p_c * (d_c - row_dot)).astype(BF16)
    yield
    dv_p = dot(low_p, weighted, nn)
    dk_p = dot(ds_p, query, nn) * scale
    grad_ref[:, pl.ds(key_col, HD)] += dk_p
    grad_ref[:, pl.ds(val_col, HD)] += dv_p
    dk_c = (dot(ds_c, query, nn) * scale).astype(BF16)
    dv_c = dot(low_c, weighted, nn).astype(BF16)
    dq = ((dot(prompt_k, ds_p, tn) + dot(comp_k, ds_c, tn)) * scale).T.astype(BF16)
    return dq, dk_c, dv_c


def chunk_kernel(
    blocks, info, q0, k0, v0, g0, q1, k1, v1, g1, w_ref, *rest
):
    prompt_refs, (out0, out1, kept, *sent, grad_ref, codes_ref) = rest[:NX], rest[NX:]
    head = pl.program_id(0)
    slots = w_ref.shape[0] // 2
    rows = kept.shape[0]
    grad_ref[...] = jnp.zeros_like(grad_ref)

    @pl.when(head == 0)
    def _():
        codes_ref[...] = jnp.zeros_like(codes_ref)

    sides = ((q0, k0, v0, g0), (q1, k1, v1, g1))
    runs = []
    for slot in range(slots):
        for side, (q, k, v, g) in enumerate(sides):
            entry = info[1 + side * slots + slot]
            run = backward_pair(
                jnp.maximum(entry, 0),
                entry >= 0,
                q[slot],
                k[slot],
                v[slot],
                g[slot],
                w_ref[side * slots + slot],
                prompt_refs,
                blocks,
                grad_ref,
            )
            runs.append((run, (out0, out1)[side], slot))
    for time in range(len(runs) + STAGES - 1):
        for start, (run, out, slot) in enumerate(runs):
            if 0 <= time - start < STAGES:
                try:
                    next(run)
                except StopIteration as stop:
                    for index, value in enumerate(stop.value):
                        out[slot, index] = value

    kept[...] = grad_ref[:rows]
    lane = lax.broadcasted_iota(jnp.int32, (8, HD), 1)
    for index, ref in enumerate(sent):
        part = slice((index + 1) * rows, (index + 2) * rows)
        codes = codes_ref[index]
        for tile in range(4):
            value, code = to_steps(grad_ref[part, tile * HD : (tile + 1) * HD])
            ref[:, pl.ds(pl.multiple_of(head * (4 * HD) + tile * HD, HD), HD)] = value
            codes = jnp.where(lane == head * 4 + tile, code, codes)
        codes_ref[index] = codes
        ref[:, ref.shape[1] - HD :] = code_rows(codes, rows)


def chunk_backward(first, heads, place, blocks, info, queries, comp, grads, other, weights, prompt_parts):
    slots, length, width = queries.shape
    half = width // HD // 2
    rows = prompt_parts[0].shape[0]
    keys = rows * NX

    def own(offset):
        return pl.BlockSpec(
            (slots, length, HD), lambda h, info: (0, 0, offset + info[0] * half + first + h)
        )

    def sent(offset):
        return pl.BlockSpec((slots, length, HD), lambda h, info: (0, 0, offset * half + first + h))

    result = pl.BlockSpec((slots, 3, length, HD), lambda h, info: (0, 0, 0, h))
    cols = heads * 4 * HD + HD
    piece = pl.BlockSpec((rows, cols), lambda h, info: (0, 0))
    kept = pl.BlockSpec((rows, 4 * HD), lambda h, info: (0, h))
    grid_spec = pltpu.PrefetchScalarGridSpec(
        num_scalar_prefetch=1,
        grid=(heads,),
        in_specs=[
            own(0),
            own(0),
            own(2 * half),
            own(0),
            sent(0),
            sent(1),
            sent(2),
            sent(3),
            pl.BlockSpec(weights.shape, lambda h, info: (0, 0, 0)),
        ]
        + [pl.BlockSpec((rows, 4 * HD), lambda h, info: (0, place + h))] * NX,
        scratch_shapes=[pltpu.VMEM((keys, 4 * HD), F32), pltpu.VMEM((NX - 1, 8, HD), F32)],
        out_specs=[result, result, kept] + [piece] * (NX - 1),
    )
    slot_shape = jax.ShapeDtypeStruct((slots, 3, length, heads * HD), BF16)
    kept_shape = jax.ShapeDtypeStruct((rows, heads * 4 * HD), F32)
    piece_shape = jax.ShapeDtypeStruct((rows, cols), I16)
    count = heads * slots * 2
    return pl.pallas_call(
        functools.partial(chunk_kernel, blocks),
        grid_spec=grid_spec,
        out_shape=[slot_shape, slot_shape, kept_shape] + [piece_shape] * (NX - 1),
        compiler_params=pltpu.CompilerParams(
            dimension_semantics=("arbitrary",), vmem_limit_bytes=VMEM_BYTES
        ),
        cost_estimate=pl.CostEstimate(
            flops=count * 24 * (keys + length) * length * HD,
            bytes_accessed=count * 7 * length * HD * 2 + heads * keys * 4 * HD * 6,
            transcendentals=count * (keys + length) * length,
        ),
        name="head_chunk",
    )(info, queries, comp, comp, grads, other, other, other, other, weights, *prompt_parts)


def half_kernel(core_ref, *refs):
    out_ref, size = refs[-1], refs[0].shape[2]
    for index, ref in enumerate(refs[:-1]):
        out_ref[:, :, index * size : (index + 1) * size] = ref[...]


def other_half(core, queries, comp, grads):
    slots, length, width = queries.shape
    half = width // 2

    def block(first):
        return pl.BlockSpec((1, length, half), lambda s, core: (s, 0, first + 1 - core[0]))

    return pl.pallas_call(
        half_kernel,
        grid_spec=pltpu.PrefetchScalarGridSpec(
            num_scalar_prefetch=1,
            grid=(slots,),
            in_specs=[block(0), block(0), block(2), block(0)],
            out_specs=pl.BlockSpec((1, length, 4 * half), lambda s, core: (s, 0, 0)),
        ),
        out_shape=jax.ShapeDtypeStruct((slots, length, 4 * half), BF16),
        compiler_params=pltpu.CompilerParams(
            dimension_semantics=("arbitrary",), vmem_limit_bytes=MOST_BYTES
        ),
        cost_estimate=pl.CostEstimate(
            flops=0, bytes_accessed=slots * length * half * 16, transcendentals=0
        ),
        name="other_half",
    )(core[None], queries, comp, comp, grads)


def place_kernel(core_ref, *refs):
    parts, out = refs[:-1], refs[-1]
    count = len(parts) // 2
    half = out.shape[2] // 2
    core = core_ref[0]
    for side, group in ((core, parts[:count]), (1 - core, parts[count:])):
        first = 0
        for part in group:
            size = part.shape[3]
            start = pl.multiple_of(side * half + first, HD)
            out[0, :, pl.ds(start, size)] = part[0, 0]
            first += size


def place_slots(core, mine, got, width, first, kinds):
    slots, _, length, _ = mine[0].shape
    total = slots * kinds * length * width * 2
    return pl.pallas_call(
        place_kernel,
        grid=(slots, kinds),
        in_specs=[pl.BlockSpec(memory_space=pltpu.SMEM)]
        + [
            pl.BlockSpec((1, 1, length, part.shape[3]), lambda s, k: (s, first + k, 0, 0))
            for part in (*mine, *got)
        ],
        out_specs=pl.BlockSpec((1, length, width), lambda s, k: (s, 0, k)),
        out_shape=jax.ShapeDtypeStruct((slots, length, kinds * width), BF16),
        cost_estimate=pl.CostEstimate(flops=0, bytes_accessed=2 * total, transcendentals=0),
        name="place_slots",
    )(core[None], *mine, *got)


def sum_kernel(counts, coded, *refs):
    ins, outs, codes_ref = refs[: 7 * len(counts)], refs[7 * len(counts) : -1], refs[-1]
    rows = outs[0].shape[0]
    head = pl.program_id(0)
    lane = lax.broadcasted_iota(jnp.int32, (16, HD), 1)

    @pl.when(head == 0)
    def _():
        codes_ref[...] = jnp.zeros_like(codes_ref)

    def add(first, kept, arrived, codes):
        powers = [jnp.exp2(code[:16].astype(F32)) * (1.0 / STEPS) for code in codes]
        for tile in range(4):
            cols = slice(tile * HD, (tile + 1) * HD)
            total = kept[:, cols]
            here = lane == (head - first) * 4 + tile
            for ref, power in zip(arrived, powers):
                scale = jnp.sum(jnp.where(here, power, 0.0), axis=1, keepdims=True)
                total += ref[:, cols].astype(F32) * scale[:1]
            for i, out in enumerate(outs):
                value = total[i * rows : (i + 1) * rows]
                if not coded or i == 0:
                    out[:, cols] = value
                    continue
                value, code = to_steps(value)
                start = pl.multiple_of(head * (4 * HD) + tile * HD, HD)
                out[:, pl.ds(start, HD)] = value
                codes_ref[i - 1] = jnp.where(lane[:8] == head * 4 + tile, code, codes_ref[i - 1])

    first = 0
    for index, heads in enumerate(counts):
        kept, *others = ins[7 * index : 7 * index + 7]

        @pl.when((head >= first) & (head < first + heads))
        def _(first=first, kept=kept, others=others):
            add(first, kept, others[:3], others[3:])

        first += heads
    if coded:
        for i, out in enumerate(outs[1:]):
            out[:, out.shape[1] - HD :] = code_rows(codes_ref[i], rows)


def sum_parts(chunks, parts, coded):
    counts = [heads for heads, _, _ in chunks]
    total = sum(counts)
    all_rows = chunks[0][1].shape[0]
    rows, cols = all_rows // parts, total * 4 * HD
    ins, in_specs = [], []
    first = 0
    for heads, kept, arrived in chunks:
        ins += [kept, *arrived, *arrived]

        def column(h, first=first, heads=heads):
            return (0, jnp.clip(h - first, 0, heads - 1))

        def last(h, heads=heads):
            return (0, heads * 4)

        in_specs += [pl.BlockSpec((all_rows, 4 * HD), column)] * 4
        in_specs += [pl.BlockSpec((all_rows, HD), last)] * 3
        first += heads
    plain = jax.ShapeDtypeStruct((rows, cols), F32)
    out_spec = pl.BlockSpec((rows, 4 * HD), lambda h: (0, h))
    other, other_spec = plain, out_spec
    if coded:
        other = jax.ShapeDtypeStruct((rows, cols + HD), I16)
        other_spec = pl.BlockSpec((rows, cols + HD), lambda h: (0, 0))
    return pl.pallas_call(
        functools.partial(sum_kernel, counts, coded),
        grid=(total,),
        in_specs=in_specs,
        out_specs=[out_spec] + [other_spec] * (parts - 1),
        out_shape=[plain] + [other] * (parts - 1),
        scratch_shapes=[pltpu.VMEM((NX - 1, 8, HD), F32)],
        compiler_params=pltpu.CompilerParams(
            dimension_semantics=("arbitrary",), vmem_limit_bytes=SMALL_BYTES
        ),
        cost_estimate=pl.CostEstimate(
            flops=0, bytes_accessed=rows * parts * cols * 14, transcendentals=0
        ),
        name="sum_parts",
    )(*ins)


def share_kernel(core_ref, mine_ref, got_ref, out_ref):
    core_first = core_ref[0] == 0
    heads = mine_ref.shape[1] // (4 * HD)
    for head in range(heads):
        for prompt in range(2):
            for kind in range(2):
                begin = (head * 4 + prompt * 2 + kind) * HD
                mine, got = mine_ref[:, begin : begin + HD], got_ref[:, begin : begin + HD]
                low, high = jnp.where(core_first, mine, got), jnp.where(core_first, got, mine)
                for side, value in enumerate((low, high)):
                    start = ((kind * 2 + side) * heads + head) * HD
                    out_ref[:, prompt, start : start + HD] = value


def place_share(core, mine, got):
    rows, width = mine.shape
    vmem = pl.BlockSpec(memory_space=pltpu.VMEM)
    return pl.pallas_call(
        share_kernel,
        in_specs=[pl.BlockSpec(memory_space=pltpu.SMEM), vmem, vmem],
        out_specs=vmem,
        out_shape=jax.ShapeDtypeStruct((rows, 2, width), F32),
        name="place_share",
    )(core[None], mine, got)


def three_parts(value):
    parts = []
    for _ in range(3):
        part = lax.reduce_precision(value, 8, 7)
        parts.append(part.astype(BF16))
        value = value - part
    return parts


def per_device(
    prompt_kv, queries, completion_kv, out_grad, rewards, token_mask, sample_lists, prompt_samples
):
    myself = lax.axis_index("samp")
    core = lax.rem(myself, 2)
    prompt_kv, queries, comp, grads = prompt_kv[0], queries[0], completion_kv[0], out_grad[0]
    slots, length, width = queries.shape
    half_width = width // 2
    half_heads = half_width // HD
    own_rows, prompts = prompt_kv.shape[0], prompt_kv.shape[1]

    lists_all = sample_lists[0]
    my_list = lax.dynamic_index_in_dim(lists_all, myself, 0, keepdims=False)
    lists = jnp.concatenate(
        [my_list, lax.dynamic_index_in_dim(lists_all, myself + 1 - 2 * core, 0, keepdims=False)]
    )
    live = (lists >= 0).astype(F32)
    member = (lists[:, None] == jnp.arange(prompts, dtype=jnp.int32)[None, :]).astype(F32)
    my_masks = token_mask[0].astype(F32)
    counts = jnp.stack(
        [jnp.sum(jnp.sum(my_masks, axis=1) * live[:slots]), jnp.sum(live[:slots])]
    )
    counts = sum_axis(jnp.broadcast_to(jnp.pad(counts, (0, 6))[:, None], (8, HD)), "dp")[:2, 0]
    my_stats = jnp.concatenate([jnp.sum(member[:slots] * rewards[0][:, None], axis=0), counts])

    facts = jnp.concatenate([my_masks, jnp.broadcast_to(rewards[0][:, None], (slots, length))], axis=0)
    facts_other = jnp.concatenate(
        [facts, jnp.pad(my_stats, (0, length - my_stats.shape[0]))[None, :]], axis=0
    )
    facts_other = move_core(facts_other)
    masks = jnp.concatenate([my_masks, facts_other[:slots]], axis=0)
    reward = jnp.concatenate([facts[slots:, 0], facts_other[slots : 2 * slots, 0]])
    stats = my_stats + facts_other[2 * slots, : prompts + 2]
    stats = jnp.concatenate(three_parts(stats))
    stats = jnp.pad(stats[None, :], ((0, 2 * own_rows - 1), (0, HD - stats.shape[0])))

    kv_heads = prompt_kv.reshape(own_rows, prompts, 2, 2, half_heads, HD)
    kv_heads = jnp.transpose(kv_heads, (3, 0, 4, 1, 2, 5)).reshape(2, own_rows, -1)
    kv_mine = lax.dynamic_index_in_dim(kv_heads, core, 0, keepdims=False)
    kv_sent = lax.dynamic_index_in_dim(kv_heads, 1 - core, 0, keepdims=False)
    kv_other = move_core(kv_sent)

    block = jnp.concatenate([kv_mine, kv_other], axis=0)

    edge = CHUNKS[0] * 4 * HD
    early = jnp.concatenate([block[:, :edge], stats], axis=1)
    near = gather_axis(early, "y")
    beside = gather_axis(block[:, edge:], "x")

    other = other_half(core, queries, comp, grads)
    other, near, beside = lax.optimization_barrier((other, near, beside))
    other = move_core(other)
    late = jnp.concatenate(beside, axis=0)

    early = gather_axis(jnp.concatenate(near, axis=0), "x")
    stats = jnp.sum(sum(value[:, edge:].astype(F32) for value in early), axis=0)
    stats = jnp.sum(stats[: 3 * (prompts + 2)].reshape(3, prompts + 2), axis=0)
    reward_mean = stats[:prompts] / prompt_samples[0].astype(F32)
    advantage = reward - jnp.sum(member * reward_mean[None, :], axis=1)
    factor = length * stats[prompts + 1] / stats[prompts]
    weights = masks * advantage[:, None] * factor
    weights = jnp.broadcast_to(weights[:, :, None], (2 * slots, length, HD))

    info = jnp.concatenate([core[None], lists]).astype(jnp.int32)
    info, late = lax.optimization_barrier((info, late))
    late = gather_axis(late, "y")
    straight = list(range(BLOCKS))
    turned = [i * NX + j for j in range(NX) for i in range(NY)]
    mine_parts, other_parts, waiting = [], [], []
    first = 0
    for heads in CHUNKS:
        early_chunk = first == 0
        outs = chunk_backward(
            first,
            heads,
            0 if early_chunk else first - CHUNKS[0],
            straight if early_chunk else turned,
            info,
            queries,
            comp,
            grads,
            other,
            weights,
            early if early_chunk else late,
        )
        first += heads
        mine, theirs, kept, *sent = outs
        if early_chunk:
            late, kept, sent, theirs = lax.optimization_barrier((late, kept, sent, theirs))
        else:
            count, *arrived = waiting.pop()
            arrived, moved, kept, sent, theirs = lax.optimization_barrier(
                (arrived, other_parts.pop(), kept, sent, theirs)
            )
            other_parts.append(moved)
            waiting.append((count, *arrived))
        info, _ = lax.optimization_barrier((info, kept))
        mine_parts.append(mine)
        arrived = [move_axis(value, "x", -step) for step, value in enumerate(sent, 1)]
        waiting.append((heads, kept, arrived))
        other_parts.append(move_core(theirs))

    comp_out = place_slots(core, mine_parts, other_parts, width, 1, 2)
    count, kept, arrived = waiting.pop()
    line = sum_parts(waiting, NY, True)
    near = [move_axis(line[step], "y", -step) for step in (1, 3)]
    arrived, near, far, comp_out = lax.optimization_barrier((arrived, near, line[2], comp_out))
    back = [near[0], move_axis(far, "y", -2), near[1]]
    last = list(sum_parts([(count, kept, arrived)], NY, True))
    last_back = [move_axis(last[step], "y", -step) for step in (1, 2, 3)]
    later_core, last[0] = lax.optimization_barrier((core, last[0]))
    query_out = place_slots(later_core, mine_parts, other_parts, width, 0, 1)
    last_back, query_out = lax.optimization_barrier((last_back, query_out))
    ends = [(half_heads - count, line[0], back), (count, last[0], last_back)]
    mine, theirs = sum_parts(ends, 2, False)
    share = place_share(core, mine, move_core(theirs))
    return (query_out[None], comp_out[None], share[None])


def solution(mesh):
    in_specs = (
        P("dp", "samp", None, None),
        P("dp", "samp", None, None),
        P("dp", "samp", None, None),
        P("dp", "samp", None, None),
        P("dp", "samp"),
        P("dp", "samp", None),
        P("dp", None, None),
        P("dp", None),
    )
    out_specs = (
        P("dp", "samp", None, None),
        P("dp", "samp", None, None),
        P("dp", "samp", None, None),
    )
    return jax.shard_map(
        per_device, mesh=mesh, in_specs=in_specs, out_specs=out_specs, check_vma=False
    )
```

```python
import functools
import math

import jax
import jax.numpy as jnp
from jax import lax
from jax.experimental import pallas as pl
from jax.experimental.pallas import tpu as pltpu
from jax.sharding import PartitionSpec as P

HD = 128
NX, NY, NC = 4, 4, 2
CHUNKS = (3, 3, 2)
BLOCKS = NX * NY
STEPS = 32760.0
STAGES = 5
VMEM_BYTES = 48 * 1024 * 1024
SMALL_BYTES = 32 * 1024 * 1024
MOST_BYTES = 60 * 1024 * 1024
F32 = jnp.float32
BF16 = jnp.bfloat16
I16 = jnp.int16


def shift_pairs(dx, dy, dc):
    pairs = []
    for x in range(NX):
        for y in range(NY):
            for c in range(NC):
                to_x, to_y, to_c = (x + dx) % NX, (y + dy) % NY, (c + dc) % NC
                pairs.append(((x * NY + y) * NC + c, (to_x * NY + to_y) * NC + to_c))
    return pairs


def move_core(value):
    return lax.ppermute(value, "samp", shift_pairs(0, 0, 1))


def move_axis(value, axis, step):
    if axis == "x":
        return lax.ppermute(value, "samp", shift_pairs(step, 0, 0))
    if axis == "y":
        return lax.ppermute(value, "samp", shift_pairs(0, step, 0))
    return lax.ppermute(value, "dp", [(i, (i + step) % 4) for i in range(4)])


def gather_axis(value, axis):
    return [value] + [move_axis(value, axis, step) for step in (1, 2, 3)]


def sum_axis(value, axis):
    first, second, third, fourth = gather_axis(value, axis)
    return (first + second) + (third + fourth)


def to_steps(value):
    peak = jnp.max(jnp.max(jnp.abs(value), axis=0, keepdims=True), axis=1, keepdims=True)
    code = jnp.floor(jnp.log2(jnp.clip(peak, 1e-30, 1e30))) + 1.0
    steps = jnp.floor(value * (jnp.exp2(-code) * STEPS) + 0.5)
    return steps.astype(jnp.int32).astype(I16), code


def code_rows(codes, rows):
    return jnp.broadcast_to(codes[:1], (rows, HD)).astype(jnp.int32).astype(I16)


def backward_pair(prompt, live, query, comp_k, comp_v, grad, weight, prompt_refs, blocks, grad_ref):
    scale = HD**-0.5
    base2 = scale * math.log2(math.e)
    nt = (((1,), (1,)), ((), ()))
    tn = (((0,), (0,)), ((), ()))
    nn = (((1,), (0,)), ((), ()))

    def dot(a, b, dims):
        return lax.dot_general(a, b, dims, preferred_element_type=F32)

    key_col = pl.multiple_of(prompt * (2 * HD), 2 * HD)
    val_col = pl.multiple_of(prompt * (2 * HD) + HD, HD)
    size = prompt_refs[0].shape[0] * len(prompt_refs) // BLOCKS

    def prompt_rows(col):
        parts = []
        for block in blocks:
            ref, place = prompt_refs[block // NX], block % NX
            parts.append(ref[place * size : (place + 1) * size, pl.ds(col, HD)])
        return jnp.concatenate(parts, axis=0)

    prompt_k, prompt_v = prompt_rows(key_col), prompt_rows(val_col)
    query = jnp.where(live, query, jnp.zeros_like(query))
    weighted = (grad.astype(F32) * weight).astype(BF16)
    weighted = jnp.where(live, weighted, jnp.zeros_like(weighted))

    s_p = dot(prompt_k, query, nt)
    s_c = dot(comp_k, query, nt)
    yield
    peak = jnp.maximum(jnp.max(s_p, axis=0, keepdims=True), jnp.max(s_c, axis=0, keepdims=True))
    peak = peak * base2
    e_p = jnp.exp2(s_p * base2 - peak)
    e_c = jnp.exp2(s_c * base2 - peak)
    total = jnp.sum(e_p, axis=0, keepdims=True) + jnp.sum(e_c, axis=0, keepdims=True)
    inverse = 1.0 / total
    p_p = e_p * inverse
    p_c = e_c * inverse
    low_p = p_p.astype(BF16)
    low_c = p_c.astype(BF16)
    yield
    d_p = dot(prompt_v, weighted, nt)
    d_c = dot(comp_v, weighted, nt)
    row_dot = jnp.sum(low_p.astype(F32) * d_p, axis=0, keepdims=True) + jnp.sum(
        low_c.astype(F32) * d_c, axis=0, keepdims=True
    )
    yield
    ds_p = (p_p * (d_p - row_dot)).astype(BF16)
    ds_c = (p_c * (d_c - row_dot)).astype(BF16)
    yield
    dv_p = dot(low_p, weighted, nn)
    dk_p = dot(ds_p, query, nn) * scale
    grad_ref[:, pl.ds(key_col, HD)] += dk_p
    grad_ref[:, pl.ds(val_col, HD)] += dv_p
    dk_c = (dot(ds_c, query, nn) * scale).astype(BF16)
    dv_c = dot(low_c, weighted, nn).astype(BF16)
    dq = ((dot(prompt_k, ds_p, tn) + dot(comp_k, ds_c, tn)) * scale).T.astype(BF16)
    return dq, dk_c, dv_c


def chunk_kernel(
    blocks, info, q0, k0, v0, g0, q1, k1, v1, g1, w_ref, *rest
):
    prompt_refs, (out0, out1, kept, *sent, grad_ref, codes_ref) = rest[:NX], rest[NX:]
    head = pl.program_id(0)
    slots = w_ref.shape[0] // 2
    rows = kept.shape[0]
    grad_ref[...] = jnp.zeros_like(grad_ref)

    @pl.when(head == 0)
    def _():
        codes_ref[...] = jnp.zeros_like(codes_ref)

    sides = ((q0, k0, v0, g0), (q1, k1, v1, g1))
    runs = []
    for slot in range(slots):
        for side, (q, k, v, g) in enumerate(sides):
            entry = info[1 + side * slots + slot]
            run = backward_pair(
                jnp.maximum(entry, 0),
                entry >= 0,
                q[slot],
                k[slot],
                v[slot],
                g[slot],
                w_ref[side * slots + slot],
                prompt_refs,
                blocks,
                grad_ref,
            )
            runs.append((run, (out0, out1)[side], slot))
    for time in range(len(runs) + STAGES - 1):
        for start, (run, out, slot) in enumerate(runs):
            if 0 <= time - start < STAGES:
                try:
                    next(run)
                except StopIteration as stop:
                    for index, value in enumerate(stop.value):
                        out[slot, index] = value

    kept[...] = grad_ref[:rows]
    lane = lax.broadcasted_iota(jnp.int32, (8, HD), 1)
    for index, ref in enumerate(sent):
        part = slice((index + 1) * rows, (index + 2) * rows)
        codes = codes_ref[index]
        for tile in range(4):
            value, code = to_steps(grad_ref[part, tile * HD : (tile + 1) * HD])
            ref[:, pl.ds(pl.multiple_of(head * (4 * HD) + tile * HD, HD), HD)] = value
            codes = jnp.where(lane == head * 4 + tile, code, codes)
        codes_ref[index] = codes
        ref[:, ref.shape[1] - HD :] = code_rows(codes, rows)


def chunk_backward(first, heads, place, blocks, info, queries, comp, grads, other, weights, prompt_parts):
    slots, length, width = queries.shape
    half = width // HD // 2
    rows = prompt_parts[0].shape[0]
    keys = rows * NX

    def own(offset):
        return pl.BlockSpec(
            (slots, length, HD), lambda h, info: (0, 0, offset + info[0] * half + first + h)
        )

    def sent(offset):
        return pl.BlockSpec((slots, length, HD), lambda h, info: (0, 0, offset * half + first + h))

    result = pl.BlockSpec((slots, 3, length, HD), lambda h, info: (0, 0, 0, h))
    cols = heads * 4 * HD + HD
    piece = pl.BlockSpec((rows, cols), lambda h, info: (0, 0))
    kept = pl.BlockSpec((rows, 4 * HD), lambda h, info: (0, h))
    grid_spec = pltpu.PrefetchScalarGridSpec(
        num_scalar_prefetch=1,
        grid=(heads,),
        in_specs=[
            own(0),
            own(0),
            own(2 * half),
            own(0),
            sent(0),
            sent(1),
            sent(2),
            sent(3),
            pl.BlockSpec(weights.shape, lambda h, info: (0, 0, 0)),
        ]
        + [pl.BlockSpec((rows, 4 * HD), lambda h, info: (0, place + h))] * NX,
        scratch_shapes=[pltpu.VMEM((keys, 4 * HD), F32), pltpu.VMEM((NX - 1, 8, HD), F32)],
        out_specs=[result, result, kept] + [piece] * (NX - 1),
    )
    slot_shape = jax.ShapeDtypeStruct((slots, 3, length, heads * HD), BF16)
    kept_shape = jax.ShapeDtypeStruct((rows, heads * 4 * HD), F32)
    piece_shape = jax.ShapeDtypeStruct((rows, cols), I16)
    count = heads * slots * 2
    return pl.pallas_call(
        functools.partial(chunk_kernel, blocks),
        grid_spec=grid_spec,
        out_shape=[slot_shape, slot_shape, kept_shape] + [piece_shape] * (NX - 1),
        compiler_params=pltpu.CompilerParams(
            dimension_semantics=("arbitrary",), vmem_limit_bytes=VMEM_BYTES
        ),
        cost_estimate=pl.CostEstimate(
            flops=count * 24 * (keys + length) * length * HD,
            bytes_accessed=count * 7 * length * HD * 2 + heads * keys * 4 * HD * 6,
            transcendentals=count * (keys + length) * length,
        ),
        name="head_chunk",
    )(info, queries, comp, comp, grads, other, other, other, other, weights, *prompt_parts)


def half_kernel(core_ref, *refs):
    out_ref, size = refs[-1], refs[0].shape[2]
    for index, ref in enumerate(refs[:-1]):
        out_ref[:, :, index * size : (index + 1) * size] = ref[...]


def other_half(core, queries, comp, grads):
    slots, length, width = queries.shape
    half = width // 2

    def block(first):
        return pl.BlockSpec((1, length, half), lambda s, core: (s, 0, first + 1 - core[0]))

    return pl.pallas_call(
        half_kernel,
        grid_spec=pltpu.PrefetchScalarGridSpec(
            num_scalar_prefetch=1,
            grid=(slots,),
            in_specs=[block(0), block(0), block(2), block(0)],
            out_specs=pl.BlockSpec((1, length, 4 * half), lambda s, core: (s, 0, 0)),
        ),
        out_shape=jax.ShapeDtypeStruct((slots, length, 4 * half), BF16),
        compiler_params=pltpu.CompilerParams(
            dimension_semantics=("arbitrary",), vmem_limit_bytes=MOST_BYTES
        ),
        cost_estimate=pl.CostEstimate(
            flops=0, bytes_accessed=slots * length * half * 16, transcendentals=0
        ),
        name="other_half",
    )(core[None], queries, comp, comp, grads)


def place_kernel(core_ref, *refs):
    parts, out = refs[:-1], refs[-1]
    count = len(parts) // 2
    half = out.shape[2] // 2
    core = core_ref[0]
    for side, group in ((core, parts[:count]), (1 - core, parts[count:])):
        first = 0
        for part in group:
            size = part.shape[3]
            start = pl.multiple_of(side * half + first, HD)
            out[0, :, pl.ds(start, size)] = part[0, 0]
            first += size


def place_slots(core, mine, got, width, first, kinds):
    slots, _, length, _ = mine[0].shape
    total = slots * kinds * length * width * 2
    return pl.pallas_call(
        place_kernel,
        grid=(slots, kinds),
        in_specs=[pl.BlockSpec(memory_space=pltpu.SMEM)]
        + [
            pl.BlockSpec((1, 1, length, part.shape[3]), lambda s, k: (s, first + k, 0, 0))
            for part in (*mine, *got)
        ],
        out_specs=pl.BlockSpec((1, length, width), lambda s, k: (s, 0, k)),
        out_shape=jax.ShapeDtypeStruct((slots, length, kinds * width), BF16),
        cost_estimate=pl.CostEstimate(flops=0, bytes_accessed=2 * total, transcendentals=0),
        name="place_slots",
    )(core[None], *mine, *got)


def sum_kernel(counts, coded, *refs):
    ins, outs, codes_ref = refs[: 7 * len(counts)], refs[7 * len(counts) : -1], refs[-1]
    rows, tiles = outs[0].shape[0], outs[0].shape[1] // HD
    head = pl.program_id(0)
    lane = lax.broadcasted_iota(jnp.int32, (16, HD), 1)

    @pl.when(head == 0)
    def _():
        codes_ref[...] = jnp.zeros_like(codes_ref)

    def add(first, kept, arrived, codes):
        powers = [jnp.exp2(code[:16].astype(F32)) * (1.0 / STEPS) for code in codes]
        for tile in range(tiles):
            cols = slice(tile * HD, (tile + 1) * HD)
            total = kept[:, cols]
            here = lane == (head - first) * tiles + tile
            for ref, power in zip(arrived, powers):
                scale = jnp.sum(jnp.where(here, power, 0.0), axis=1, keepdims=True)
                total += ref[:, cols].astype(F32) * scale[:1]
            for i, out in enumerate(outs):
                value = total[i * rows : (i + 1) * rows]
                if not coded or i == 0:
                    out[:, cols] = value
                    continue
                value, code = to_steps(value)
                start = pl.multiple_of(head * (tiles * HD) + tile * HD, HD)
                out[:, pl.ds(start, HD)] = value
                codes_ref[i - 1] = jnp.where(lane[:8] == head * tiles + tile, code, codes_ref[i - 1])

    first = 0
    for index, heads in enumerate(counts):
        kept, *others = ins[7 * index : 7 * index + 7]

        @pl.when((head >= first) & (head < first + heads))
        def _(first=first, kept=kept, others=others):
            add(first, kept, others[:3], others[3:])

        first += heads
    if coded:
        for i, out in enumerate(outs[1:]):
            out[:, out.shape[1] - HD :] = code_rows(codes_ref[i], rows)


def sum_parts(chunks, parts, coded):
    group = math.gcd(*[heads for heads, _, _ in chunks])
    counts = [heads // group for heads, _, _ in chunks]
    total = sum(counts)
    step = group * 4 * HD
    all_rows = chunks[0][1].shape[0]
    rows, cols = all_rows // parts, total * step
    ins, in_specs = [], []
    first = 0
    for heads, kept, arrived in chunks:
        ins += [kept, *arrived, *arrived]

        def column(h, first=first, count=heads // group):
            return (0, jnp.clip(h - first, 0, count - 1))

        def last(h, heads=heads):
            return (0, heads * 4)

        in_specs += [pl.BlockSpec((all_rows, step), column)] * 4
        in_specs += [pl.BlockSpec((all_rows, HD), last)] * 3
        first += heads // group
    plain = jax.ShapeDtypeStruct((rows, cols), F32)
    out_spec = pl.BlockSpec((rows, step), lambda h: (0, h))
    other, other_spec = plain, out_spec
    if coded:
        other = jax.ShapeDtypeStruct((rows, cols + HD), I16)
        other_spec = pl.BlockSpec((rows, cols + HD), lambda h: (0, 0))
    return pl.pallas_call(
        functools.partial(sum_kernel, counts, coded),
        grid=(total,),
        in_specs=in_specs,
        out_specs=[out_spec] + [other_spec] * (parts - 1),
        out_shape=[plain] + [other] * (parts - 1),
        scratch_shapes=[pltpu.VMEM((NX - 1, 8, HD), F32)],
        compiler_params=pltpu.CompilerParams(
            dimension_semantics=("arbitrary",), vmem_limit_bytes=SMALL_BYTES
        ),
        cost_estimate=pl.CostEstimate(
            flops=0, bytes_accessed=rows * parts * cols * 14, transcendentals=0
        ),
        name="sum_parts",
    )(*ins)


def share_kernel(core_ref, mine_ref, got_ref, out_ref):
    core_first = core_ref[0] == 0
    heads = mine_ref.shape[1] // (4 * HD)
    for head in range(heads):
        for prompt in range(2):
            for kind in range(2):
                begin = (head * 4 + prompt * 2 + kind) * HD
                mine, got = mine_ref[:, begin : begin + HD], got_ref[:, begin : begin + HD]
                low, high = jnp.where(core_first, mine, got), jnp.where(core_first, got, mine)
                for side, value in enumerate((low, high)):
                    start = ((kind * 2 + side) * heads + head) * HD
                    out_ref[:, prompt, start : start + HD] = value


def place_share(core, mine, got):
    rows, width = mine.shape
    vmem = pl.BlockSpec(memory_space=pltpu.VMEM)
    return pl.pallas_call(
        share_kernel,
        in_specs=[pl.BlockSpec(memory_space=pltpu.SMEM), vmem, vmem],
        out_specs=vmem,
        out_shape=jax.ShapeDtypeStruct((rows, 2, width), F32),
        name="place_share",
    )(core[None], mine, got)


def three_parts(value):
    parts = []
    for _ in range(3):
        part = lax.reduce_precision(value, 8, 7)
        parts.append(part.astype(BF16))
        value = value - part
    return parts


def per_device(
    prompt_kv, queries, completion_kv, out_grad, rewards, token_mask, sample_lists, prompt_samples
):
    myself = lax.axis_index("samp")
    core = lax.rem(myself, 2)
    prompt_kv, queries, comp, grads = prompt_kv[0], queries[0], completion_kv[0], out_grad[0]
    slots, length, width = queries.shape
    half_width = width // 2
    half_heads = half_width // HD
    own_rows, prompts = prompt_kv.shape[0], prompt_kv.shape[1]

    lists_all = sample_lists[0]
    my_list = lax.dynamic_index_in_dim(lists_all, myself, 0, keepdims=False)
    lists = jnp.concatenate(
        [my_list, lax.dynamic_index_in_dim(lists_all, myself + 1 - 2 * core, 0, keepdims=False)]
    )
    live = (lists >= 0).astype(F32)
    member = (lists[:, None] == jnp.arange(prompts, dtype=jnp.int32)[None, :]).astype(F32)
    my_masks = token_mask[0].astype(F32)
    counts = jnp.stack(
        [jnp.sum(jnp.sum(my_masks, axis=1) * live[:slots]), jnp.sum(live[:slots])]
    )
    counts = sum_axis(jnp.broadcast_to(jnp.pad(counts, (0, 6))[:, None], (8, HD)), "dp")[:2, 0]
    my_stats = jnp.concatenate([jnp.sum(member[:slots] * rewards[0][:, None], axis=0), counts])

    facts = jnp.concatenate([my_masks, jnp.broadcast_to(rewards[0][:, None], (slots, length))], axis=0)
    facts_other = jnp.concatenate(
        [facts, jnp.pad(my_stats, (0, length - my_stats.shape[0]))[None, :]], axis=0
    )
    facts_other = move_core(facts_other)
    masks = jnp.concatenate([my_masks, facts_other[:slots]], axis=0)
    reward = jnp.concatenate([facts[slots:, 0], facts_other[slots : 2 * slots, 0]])
    stats = my_stats + facts_other[2 * slots, : prompts + 2]
    stats = jnp.concatenate(three_parts(stats))
    stats = jnp.pad(stats[None, :], ((0, 2 * own_rows - 1), (0, HD - stats.shape[0])))

    kv_heads = prompt_kv.reshape(own_rows, prompts, 2, 2, half_heads, HD)
    kv_heads = jnp.transpose(kv_heads, (3, 0, 4, 1, 2, 5)).reshape(2, own_rows, -1)
    kv_mine = lax.dynamic_index_in_dim(kv_heads, core, 0, keepdims=False)
    kv_sent = lax.dynamic_index_in_dim(kv_heads, 1 - core, 0, keepdims=False)
    kv_other = move_core(kv_sent)

    block = jnp.concatenate([kv_mine, kv_other], axis=0)

    edge = CHUNKS[0] * 4 * HD
    early = jnp.concatenate([block[:, :edge], stats], axis=1)
    near = gather_axis(early, "y")
    beside = gather_axis(block[:, edge:], "x")

    other = other_half(core, queries, comp, grads)
    other, near, beside = lax.optimization_barrier((other, near, beside))
    other = move_core(other)
    late = jnp.concatenate(beside, axis=0)

    early = gather_axis(jnp.concatenate(near, axis=0), "x")
    stats = jnp.sum(sum(value[:, edge:].astype(F32) for value in early), axis=0)
    stats = jnp.sum(stats[: 3 * (prompts + 2)].reshape(3, prompts + 2), axis=0)
    reward_mean = stats[:prompts] / prompt_samples[0].astype(F32)
    advantage = reward - jnp.sum(member * reward_mean[None, :], axis=1)
    factor = length * stats[prompts + 1] / stats[prompts]
    weights = masks * advantage[:, None] * factor
    weights = jnp.broadcast_to(weights[:, :, None], (2 * slots, length, HD))

    info = jnp.concatenate([core[None], lists]).astype(jnp.int32)
    info, late = lax.optimization_barrier((info, late))
    late = gather_axis(late, "y")
    straight = list(range(BLOCKS))
    turned = [i * NX + j for j in range(NX) for i in range(NY)]
    mine_parts, other_parts, waiting = [], [], []
    first = 0
    for heads in CHUNKS:
        early_chunk = first == 0
        outs = chunk_backward(
            first,
            heads,
            0 if early_chunk else first - CHUNKS[0],
            straight if early_chunk else turned,
            info,
            queries,
            comp,
            grads,
            other,
            weights,
            early if early_chunk else late,
        )
        first += heads
        mine, theirs, kept, *sent = outs
        if early_chunk:
            late, kept, sent, theirs = lax.optimization_barrier((late, kept, sent, theirs))
        else:
            count, *arrived = waiting.pop()
            arrived, moved, kept, sent, theirs = lax.optimization_barrier(
                (arrived, other_parts.pop(), kept, sent, theirs)
            )
            other_parts.append(moved)
            waiting.append((count, *arrived))
        info, _ = lax.optimization_barrier((info, kept))
        mine_parts.append(mine)
        arrived = [move_axis(value, "x", -step) for step, value in enumerate(sent, 1)]
        waiting.append((heads, kept, arrived))
        other_parts.append(move_core(theirs))

    comp_out = place_slots(core, mine_parts, other_parts, width, 1, 2)
    count, kept, arrived = waiting.pop()
    line = sum_parts(waiting, NY, True)
    near = [move_axis(line[step], "y", -step) for step in (1, 3)]
    arrived, near, far, comp_out = lax.optimization_barrier((arrived, near, line[2], comp_out))
    back = [near[0], move_axis(far, "y", -2), near[1]]
    last = list(sum_parts([(count, kept, arrived)], NY, True))
    last_back = [move_axis(last[step], "y", -step) for step in (1, 2, 3)]
    later_core, last[0] = lax.optimization_barrier((core, last[0]))
    query_out = place_slots(later_core, mine_parts, other_parts, width, 0, 1)
    last_back, query_out = lax.optimization_barrier((last_back, query_out))
    ends = [(half_heads - count, line[0], back), (count, last[0], last_back)]
    mine, theirs = sum_parts(ends, 2, False)
    share = place_share(core, mine, move_core(theirs))
    return (query_out[None], comp_out[None], share[None])


def solution(mesh):
    in_specs = (
        P("dp", "samp", None, None),
        P("dp", "samp", None, None),
        P("dp", "samp", None, None),
        P("dp", "samp", None, None),
        P("dp", "samp"),
        P("dp", "samp", None),
        P("dp", None, None),
        P("dp", None),
    )
    out_specs = (
        P("dp", "samp", None, None),
        P("dp", "samp", None, None),
        P("dp", "samp", None, None),
    )
    return jax.shard_map(
        per_device, mesh=mesh, in_specs=in_specs, out_specs=out_specs, check_vma=False
    )
```
